128 devices in a mesh: seq: 32 (over x, y, core), head: 4 (over z).
Axes of the slice: x: 4, y: 4, z: 4, core: 2. Of those that a mesh axis runs over, the one named last changes fastest.
Arguments:
- query: bfloat16 [16384, 4096], P('seq', 'head'), may hold values from -120 to 120
- key: bfloat16 [16384, 4096], P('seq', 'head'), may hold values from -6 to 6
- value: bfloat16 [16384, 4096], P('seq', 'head'), may hold values from -6 to 6
- out_weight: bfloat16 [4096, 4096], P('head'), may hold values from -0.09375 to 0.09375
Outputs:
- mixed: bfloat16 [16384, 4096], P('seq', 'head')
The draws below stay inside these ranges and needn't reach their ends.
All inputs are finite; a program needn't handle non-finite values.
Results may differ from the reference program's by a relative error of at most 0.012.
Values may be sent and summed in bfloat16 or wider, within the bound.
A program may use at most 256 MiB of HBM per device.

```python
import math
import jax
import jax.numpy as jnp
from jax import lax

D = 4096
H = 32
DH = 128
B = 256
TOKENS = 16384


def tied_keys(key, pinch):
    drawn = jax.random.truncated_normal(key, -6.0, 6.0, (TOKENS, H * DH), jnp.float32)
    row_ids = jnp.arange(TOKENS)[:, None]
    following = jnp.roll(drawn, -1, axis=0)
    marked = ((row_ids + 2) % 61 == 7) & (pinch > 0.0)
    return jnp.where(marked, pinch * following, drawn)


def draw_key(key, part):
    shared = tied_keys(key, 0.0)
    return shared.astype(jnp.bfloat16)


def draw_query(key, part):
    key = jax.random.fold_in(key, 11)
    drawn = jax.random.truncated_normal(key, -6.0, 6.0, (TOKENS, H * DH), jnp.float32)
    return drawn.astype(jnp.bfloat16)


def block_scale(own_key, dims, shards, smallest, high):
    gain = 1.0
    for axis_at, parts in shards:
        heights = jax.random.uniform(jax.random.fold_in(jax.random.fold_in(own_key, 6), axis_at), (parts,), jnp.float32, smallest / len(shards), high / len(shards))
        gain = gain * jnp.repeat(jnp.exp(heights), dims[axis_at] // parts).reshape((-1,) + (1,) * (len(dims) - 1 - axis_at))
    return gain


def gaussian(stream_key, dims, spread, bound, split=(), kind=jnp.bfloat16):
    factor_of = block_scale(stream_key, dims, split, -0.22, 0.18) if split else 1.0
    drawn = jax.random.normal(stream_key, dims, jnp.float32) * spread * factor_of
    return jnp.minimum(jnp.maximum(drawn, -bound), bound).astype(kind)


def setup_inputs(seed: int = 0) -> dict:
    arg_keys = jax.random.split(jax.random.key(seed), 5)
    query = draw_query(jax.random.fold_in(arg_keys[4], 71), 0)
    key = draw_key(jax.random.fold_in(arg_keys[4], 71), 0)
    value = gaussian(arg_keys[2], (TOKENS, H * DH), 1.0, 6.0, ((0, 32), (1, 4)))
    out_weight = gaussian(arg_keys[3], (H * DH, D), (H * DH) ** -0.5, 0.09375, ((0, 4),))
    return {"query": query, "key": key, "value": value, "out_weight": out_weight}


NEG_FILL = -1e+30
LOG_TWO = math.log(2.0)

def halve(matrix):
    paired = matrix.reshape(matrix.shape[0] // 2, 2, matrix.shape[1]).astype(jnp.float32)
    return (0.5 * (paired[:, 0] + paired[:, 1])).astype(jnp.bfloat16)

def block_bias(block, levels):
    row_ids = jnp.arange(B)[:, None]
    col_ids = jnp.arange(2 * B)[None, :]
    nearby = (col_ids < B) & (block >= 1) | (col_ids >= B) & (col_ids - B <= row_ids)
    pieces = [jnp.where(nearby, 0.0, NEG_FILL).astype(jnp.float32)]
    coarse_ids = jnp.arange(B)
    for level in range(1, levels):
        allowed = (block // 2 ** level >= 1) & (coarse_ids // (B // 2) <= block // 2 ** (level - 1) % 2)
        bias_row = jnp.where(allowed, level * LOG_TWO, NEG_FILL).astype(jnp.float32)
        pieces.append(jnp.broadcast_to(bias_row[None, :], (B, B)))
    return jnp.concatenate(pieces, 1)

def attend(queries, keys, values, bias, heads):
    query_h = queries.reshape(B, heads, DH).astype(jnp.float32)
    key_h = keys.reshape(keys.shape[0], heads, DH).astype(jnp.float32)
    value_h = values.reshape(values.shape[0], heads, DH).astype(jnp.float32)
    scores = jnp.einsum('qhd,khd->hqk', query_h, key_h) * (1.0 / math.sqrt(DH)) + bias[None]
    peak = lax.optimization_barrier(jnp.max(scores, axis=-1, keepdims=True))
    weights = jnp.exp(scores - peak)
    total = lax.optimization_barrier(jnp.sum(weights, axis=-1))
    probs = weights.astype(jnp.bfloat16).astype(jnp.float32)
    summed = jnp.einsum('hqk,khd->qhd', probs, value_h)
    return (summed / jnp.transpose(total)[:, :, None]).astype(jnp.bfloat16).reshape(B, heads * DH)

def reference(query, key, value, out_weight):
    width = H * DH
    levels = (TOKENS // B).bit_length() - 1
    key_levels = [key]
    value_levels = [value]
    for level in range(1, levels):
        key_levels.append(halve(key_levels[-1]))
        value_levels.append(halve(value_levels[-1]))
    zero_rows = jnp.zeros((B, width), jnp.bfloat16)
    key_padded = [jnp.concatenate([zero_rows, matrix], 0) for matrix in key_levels]
    value_padded = [jnp.concatenate([zero_rows, matrix], 0) for matrix in value_levels]

    def one_block(block):
        keys_list = [lax.dynamic_slice_in_dim(key_padded[0], block * B, 2 * B, 0)]
        values_list = [lax.dynamic_slice_in_dim(value_padded[0], block * B, 2 * B, 0)]
        for level in range(1, levels):
            start = (block // 2 ** level * B).astype(jnp.int32)
            keys_list.append(lax.dynamic_slice_in_dim(key_padded[level], start, B, 0))
            values_list.append(lax.dynamic_slice_in_dim(value_padded[level], start, B, 0))
        queries = lax.dynamic_slice_in_dim(query, (block * B).astype(jnp.int32), B, 0)
        return attend(queries, jnp.concatenate(keys_list, 0), jnp.concatenate(values_list, 0), block_bias(block, levels), H)
    attended = lax.map(one_block, jnp.arange(TOKENS // B, dtype=jnp.int32)).reshape(TOKENS, width)
    return jnp.dot(attended, out_weight, preferred_element_type=jnp.float32).astype(jnp.bfloat16)
```

```python
import functools
import math

import jax
import jax.numpy as jnp
from jax import lax
from jax.experimental import pallas as pl
from jax.experimental.pallas import tpu as pltpu
from jax.sharding import PartitionSpec as P

DH = 128
B = 256
HALF = 128
WIDTH = 1024
HEADS = WIDTH // DH
CHIPS = 16
PLANES = 4
NEG = -1e30
SCALE = math.log2(math.e) / math.sqrt(DH)
MESH = pl.DeviceIdType.MESH

OWN = B
COARSE = 3 * B
ROWS = 8 * B
POOLED = {1: 0, 2: 256, 3: 384, 4: 448, 5: 480}
HOPS = (2, 1, 3)


def level_at(level):
    return COARSE + (level - 1) * B


def kernel(
    q_hbm,
    k_hbm,
    v_hbm,
    w_hbm,
    out_ref,
    kv,
    pooled,
    q_ref,
    w_ref,
    attended,
    partial,
    own,
    landed,
    load_sem,
    tail_send,
    tail_recv,
    level_send,
    level_recv,
    pass_send,
    pass_recv,
    sum_send,
    sum_recv,
):
    device = lax.axis_index("seq")
    plane = lax.axis_index("head")
    chip = device // 2
    core = device % 2
    sibling = 2 * chip + (1 - core)
    first_core = core == 0
    second_core = core == 1

    loads = [
        pltpu.make_async_copy(k_hbm, kv.at[0, pl.ds(OWN, 2 * B)], load_sem.at[0]),
        pltpu.make_async_copy(v_hbm, kv.at[1, pl.ds(OWN, 2 * B)], load_sem.at[1]),
        pltpu.make_async_copy(q_hbm, q_ref, load_sem.at[2]),
        pltpu.make_async_copy(w_hbm, w_ref, load_sem.at[3]),
    ]
    for load in loads:
        load.start()

    def clear(start, rows):
        kv[:, pl.ds(start, rows), :] = jnp.zeros((2, rows, WIDTH), jnp.bfloat16)

    @pl.when(device == 0)
    def _():
        clear(0, B)
        clear(level_at(1), B)

    @pl.when(first_core)
    def _():
        clear(level_at(2) + HALF, HALF)

    @pl.when(second_core & (chip == 0))
    def _():
        clear(level_at(2), B)

    for level in (3, 4, 5):
        group = chip // 2 ** (level - 2)
        second = chip // 2 ** (level - 3) % 2

        @pl.when(second_core & (group == 0))
        def _():
            clear(level_at(level), HALF)

        @pl.when(second_core & ((group == 0) | (second == 0)))
        def _():
            clear(level_at(level) + HALF, HALF)

    barrier = pltpu.get_barrier_semaphore()

    def greet(seq_at, plane_at):
        pl.semaphore_signal(barrier, inc=1, device_id=(seq_at, plane_at), device_id_type=MESH)

    for hop in HOPS:
        greet(device, (plane + hop) % PLANES)
    greet(sibling, plane)

    @pl.when(first_core & (chip > 0))
    def _():
        greet(device - 1, plane)

    @pl.when(second_core)
    def _():
        def each(source, carry):
            greet(source, plane)
            return carry

        lax.fori_loop(0, 2 * chip, each, 0)

    following = CHIPS - 1 - chip
    more = jnp.where(second_core & (chip < CHIPS - 1), 1, 0)
    pl.semaphore_wait(barrier, len(HOPS) + 1 + following + more)

    loads[0].wait()
    loads[1].wait()

    def pool(source, rows):
        row = lax.broadcasted_iota(jnp.int32, (rows, 2 * rows), 0)
        col = lax.broadcasted_iota(jnp.int32, (rows, 2 * rows), 1)
        pairs = jnp.where((col >> 1) == row, 0.5, 0.0).astype(jnp.bfloat16)
        return jnp.dot(pairs, source, preferred_element_type=jnp.float32).astype(jnp.bfloat16)

    def pool_columns(at, carry):
        columns = pl.ds(pl.multiple_of(at * 256, 256), 256)
        for side in range(2):
            rows = kv[side, pl.ds(OWN, 2 * B), columns]
            for level in range(1, 6):
                rows = pool(rows, 512 >> level)
                pooled[side, pl.ds(POOLED[level], 512 >> level), columns] = rows
        return carry

    lax.fori_loop(0, WIDTH // 256, pool_columns, 0)

    ahead = jnp.where(first_core, sibling, jnp.minimum(device + 1, 2 * CHIPS - 1))
    tail_copy = pltpu.make_async_remote_copy(
        src_ref=kv.at[:, pl.ds(OWN + B, B)],
        dst_ref=kv.at[:, pl.ds(0, B)],
        send_sem=tail_send.at[0],
        recv_sem=tail_recv.at[0],
        device_id=(ahead, plane),
        device_id_type=MESH,
    )
    first_copy = pltpu.make_async_remote_copy(
        src_ref=pooled.at[:, pl.ds(0, B)],
        dst_ref=kv.at[:, pl.ds(level_at(1), B)],
        send_sem=tail_send.at[1],
        recv_sem=tail_recv.at[1],
        device_id=(ahead, plane),
        device_id_type=MESH,
    )

    level_copies = []
    for level in (2, 3, 4, 5):
        rows = 512 >> level
        members = 2 ** (level - 2)
        group = chip // members
        place = device - group * (2 * members)
        for member in range(members):
            target = (group + 1) * members + member
            wanted = target < CHIPS
            if level >= 3 and member < members // 2:
                wanted = wanted & (chip // 2 ** (level - 3) % 2 == 0)
            copy = pltpu.make_async_remote_copy(
                src_ref=pooled.at[:, pl.ds(POOLED[level], rows)],
                dst_ref=kv.at[:, pl.ds(pl.multiple_of(level_at(level) + place * rows, 16), rows)],
                send_sem=level_send.at[len(level_copies)],
                recv_sem=level_recv.at[level - 2],
                device_id=(2 * jnp.minimum(target, CHIPS - 1) + 1, plane),
                device_id_type=MESH,
            )
            level_copies.append((wanted, copy))

    @pl.when(first_core)
    def _():
        first_copy.start()
        tail_copy.start()

    for wanted, copy in level_copies:
        @pl.when(wanted)
        def _():
            copy.start()

    @pl.when(level_copies[0][0])
    def _():
        level_copies[0][1].wait_send()

    @pl.when(second_core & (chip < CHIPS - 1))
    def _():
        first_copy.start()
        tail_copy.start()

    def handed(index, start, rows):
        return pltpu.make_async_remote_copy(
            src_ref=kv.at[:, pl.ds(start, rows)],
            dst_ref=kv.at[:, pl.ds(start, rows)],
            send_sem=pass_send.at[index],
            recv_sem=pass_recv.at[index],
            device_id=(sibling, plane),
            device_id_type=MESH,
        )

    hand_overs = [handed(0, level_at(2), HALF)]
    for level in (3, 4, 5):
        hand_overs.append(handed(level - 2, level_at(level), B))

    def arrived(level, rows):
        whole = kv.at[:, pl.ds(level_at(level), rows)]
        pltpu.make_async_copy(whole, whole, level_recv.at[level - 2]).wait()

    for index, level in enumerate((2, 3, 4, 5)):
        if level == 2:
            @pl.when(second_core & (chip > 0))
            def _():
                arrived(2, B)
        else:
            group = chip // 2 ** (level - 2)
            second = chip // 2 ** (level - 3) % 2

            @pl.when(second_core & (group > 0) & (second == 1))
            def _():
                arrived(level, B)

            @pl.when(second_core & (group > 0) & (second == 0))
            def _():
                arrived(level, HALF)

        @pl.when(second_core)
        def _():
            hand_overs[index].start()

    loads[2].wait()
    loads[3].wait()

    @pl.when(device > 0)
    def _():
        first_copy.wait_recv()

    @pl.when(first_core)
    def _():
        for copy in hand_overs:
            copy.wait_recv()

    def nt(left, right):
        return lax.dot_general(
            left, right, (((1,), (1,)), ((), ())), preferred_element_type=jnp.float32
        )

    lower = lax.broadcasted_iota(jnp.int32, (HALF, HALF), 0) >= lax.broadcasted_iota(
        jnp.int32, (HALF, HALF), 1
    )

    def attend(block):
        beta = 2 * device + block
        rows = pl.ds(block * B, B)
        prior_bias = jnp.where(beta >= 1, 0.0, NEG)
        biases = []
        for level in range(1, 6):
            there = beta // 2**level >= 1
            whole = there & (beta // 2 ** (level - 1) % 2 == 1)
            biases.append(jnp.where(there, float(level), NEG))
            biases.append(jnp.where(whole, float(level), NEG))

        def one_head(head, carry):
            columns = pl.ds(pl.multiple_of(head * DH, DH), DH)
            queries = q_ref[rows, columns]
            pieces = []
            starts = [block * B, block * B + B] + [level_at(level) for level in range(1, 6)]
            for at, start in enumerate(starts):
                dots = nt(queries, kv[0, pl.ds(start, B), columns]) * SCALE
                left, right = dots[:, :HALF], dots[:, HALF:]
                if at == 0:
                    left, right = left + prior_bias, right + prior_bias
                elif at == 1:
                    left = jnp.concatenate([jnp.where(lower, left[:HALF], NEG), left[HALF:]], 0)
                    right = jnp.concatenate(
                        [jnp.full((HALF, HALF), NEG), jnp.where(lower, right[HALF:], NEG)], 0
                    )
                else:
                    left = left + biases[2 * at - 4]
                    right = right + biases[2 * at - 3]
                pieces += [left, right]
            peak = functools.reduce(jnp.maximum, pieces)
            peak = jnp.max(peak, axis=1, keepdims=True)
            total = jnp.zeros((B, HALF), jnp.float32)
            summed = jnp.zeros((B, DH), jnp.float32)
            for at, start in enumerate(starts):
                left = jnp.exp2(pieces[2 * at] - peak)
                right = jnp.exp2(pieces[2 * at + 1] - peak)
                total = total + left + right
                probs = jnp.concatenate([left, right], 1).astype(jnp.bfloat16)
                summed = summed + jnp.dot(
                    probs, kv[1, pl.ds(start, B), columns], preferred_element_type=jnp.float32
                )
            total = jnp.sum(total, axis=1, keepdims=True)
            attended[rows, columns] = (summed / total).astype(jnp.bfloat16)
            return carry

        lax.fori_loop(0, HEADS, one_head, 0)

    def project(block):
        rows = pl.ds(block * B, B)
        copies = []
        for index, hop in enumerate(HOPS + (0,)):
            target = (plane + hop) % PLANES

            def tile(at, carry):
                columns = pl.ds(pl.multiple_of(target * WIDTH + at * 256, 256), 256)
                here = pl.ds(pl.multiple_of(at * 256, 256), 256)
                term = jnp.dot(
                    attended[rows, :], w_ref[:, columns], preferred_element_type=jnp.float32
                )
                if hop:
                    partial[index, rows, here] = term.astype(jnp.bfloat16)
                else:
                    own[rows, here] = term
                return carry

            lax.fori_loop(0, WIDTH // 256, tile, 0)
            if hop:
                copy = pltpu.make_async_remote_copy(
                    src_ref=partial.at[index, rows],
                    dst_ref=landed.at[index, rows],
                    send_sem=sum_send.at[index, block],
                    recv_sem=sum_recv.at[index, block],
                    device_id=(device, target),
                    device_id_type=MESH,
                )
                copy.start()
                copies.append(copy)
        return copies

    attend(1)
    sum_copies = {1: project(1)}

    @pl.when(device > 0)
    def _():
        tail_copy.wait_recv()

    attend(0)
    sum_copies[0] = project(0)

    for block in (1, 0):
        rows = pl.ds(block * B, B)
        for copy in sum_copies[block]:
            copy.wait_recv()
        total = own[rows, :]
        for index in range(len(HOPS)):
            total = total + landed[index, rows, :].astype(jnp.float32)
        out_ref[rows, :] = total.astype(jnp.bfloat16)

    for block in (1, 0):
        for copy in sum_copies[block]:
            copy.wait_send()
    for at, (wanted, copy) in enumerate(level_copies):
        if at:
            @pl.when(wanted)
            def _():
                copy.wait_send()

    @pl.when(device < 2 * CHIPS - 1)
    def _():
        first_copy.wait_send()
        tail_copy.wait_send()

    @pl.when(second_core)
    def _():
        for copy in hand_overs:
            copy.wait_send()


def per_device(query, key, value, out_weight):
    tokens = query.shape[0]
    dma = pltpu.SemaphoreType.DMA
    bf16 = jnp.bfloat16
    return pl.pallas_call(
        kernel,
        out_shape=jax.ShapeDtypeStruct((tokens, WIDTH), bf16),
        in_specs=[pl.BlockSpec(memory_space=pl.ANY)] * 4,
        out_specs=pl.BlockSpec(memory_space=pltpu.VMEM),
        scratch_shapes=[
            pltpu.VMEM((2, ROWS, WIDTH), bf16),
            pltpu.VMEM((2, 512, WIDTH), bf16),
            pltpu.VMEM((tokens, WIDTH), bf16),
            pltpu.VMEM((WIDTH, PLANES * WIDTH), bf16),
            pltpu.VMEM((tokens, WIDTH), bf16),
            pltpu.VMEM((len(HOPS), tokens, WIDTH), bf16),
            pltpu.VMEM((tokens, WIDTH), jnp.float32),
            pltpu.VMEM((len(HOPS), tokens, WIDTH), bf16),
            dma((4,)),
            dma((2,)),
            dma((2,)),
            dma((15,)),
            dma((4,)),
            dma((4,)),
            dma((4,)),
            dma((len(HOPS), 2)),
            dma((len(HOPS), 2)),
        ],
        compiler_params=pltpu.CompilerParams(
            collective_id=0, has_side_effects=True, vmem_limit_bytes=56 << 20
        ),
        cost_estimate=pl.CostEstimate(
            flops=8_000_000_000, bytes_accessed=13_000_000, transcendentals=7_400_000
        ),
        name="attend_and_project",
    )(query, key, value, out_weight)


def solution(mesh):
    in_specs = (P("seq", "head"), P("seq", "head"), P("seq", "head"), P("head", None))
    out_specs = P("seq", "head")
    return jax.shard_map(
        per_device, mesh=mesh, in_specs=in_specs, out_specs=out_specs, check_vma=False
    )
```

```python
import functools
import math

import jax
import jax.numpy as jnp
from jax import lax
from jax.experimental import pallas as pl
from jax.experimental.pallas import tpu as pltpu
from jax.sharding import PartitionSpec as P

DH = 128
B = 256
HALF = 128
WIDTH = 1024
HEADS = WIDTH // DH
CHIPS = 16
PLANES = 4
NEG = -1e30
SCALE = math.log2(math.e) / math.sqrt(DH)
MESH = pl.DeviceIdType.MESH

OWN = B
COARSE = 3 * B
ROWS = 8 * B
POOLED = {1: 0, 2: 256, 3: 384, 4: 448, 5: 480}


def level_at(level):
    return COARSE + (level - 1) * B


def kernel(
    q_hbm,
    k_hbm,
    v_hbm,
    w_hbm,
    out_ref,
    kv,
    pooled,
    q_ref,
    w_own,
    w_far,
    attended,
    far,
    partial,
    own,
    landed,
    load_sem,
    tail_send,
    tail_recv,
    level_send,
    level_recv,
    pass_send,
    pass_recv,
    weight_send,
    weight_recv,
    share_send,
    share_recv,
    far_send,
    far_recv,
    sum_send,
    sum_recv,
):
    device = lax.axis_index("seq")
    plane = lax.axis_index("head")
    chip = device // 2
    core = device % 2
    sibling = 2 * chip + (1 - core)
    first_core = core == 0
    second_core = core == 1
    ally = plane + 1 - 2 * (plane % 2)
    peer = PLANES - 1 - plane

    def of_plane(at):
        return pl.ds(pl.multiple_of(at * WIDTH, WIDTH), WIDTH)

    kept = (plane, peer)
    given = (ally, PLANES - 1 - ally)

    loads = [
        pltpu.make_async_copy(k_hbm, kv.at[0, pl.ds(OWN, 2 * B)], load_sem.at[0]),
        pltpu.make_async_copy(v_hbm, kv.at[1, pl.ds(OWN, 2 * B)], load_sem.at[1]),
        pltpu.make_async_copy(q_hbm, q_ref, load_sem.at[2]),
        pltpu.make_async_copy(w_hbm.at[:, of_plane(kept[0])], w_own.at[0], load_sem.at[3]),
        pltpu.make_async_copy(w_hbm.at[:, of_plane(kept[1])], w_own.at[1], load_sem.at[4]),
    ]
    for load in loads:
        load.start()

    def clear(start, rows):
        kv[:, pl.ds(start, rows), :] = jnp.zeros((2, rows, WIDTH), jnp.bfloat16)

    @pl.when(device == 0)
    def _():
        clear(0, B)
        clear(level_at(1), B)

    @pl.when(first_core)
    def _():
        clear(level_at(2) + HALF, HALF)

    @pl.when(second_core & (chip == 0))
    def _():
        clear(level_at(2), B)

    for level in (3, 4, 5):
        group = chip // 2 ** (level - 2)
        second = chip // 2 ** (level - 3) % 2

        @pl.when(second_core & (group == 0))
        def _():
            clear(level_at(level), HALF)

        @pl.when(second_core & ((group == 0) | (second == 0)))
        def _():
            clear(level_at(level) + HALF, HALF)

    barrier = pltpu.get_barrier_semaphore()

    def greet(seq_at, plane_at):
        pl.semaphore_signal(barrier, inc=1, device_id=(seq_at, plane_at), device_id_type=MESH)

    greet(device, ally)
    greet(device, peer)
    greet(sibling, plane)

    @pl.when(first_core & (chip > 0))
    def _():
        greet(device - 1, plane)

    @pl.when(second_core)
    def _():
        def each(source, carry):
            greet(source, plane)
            return carry

        lax.fori_loop(0, 2 * chip, each, 0)

    following = CHIPS - 1 - chip
    more = jnp.where(second_core & (chip < CHIPS - 1), 1, 0)
    pl.semaphore_wait(barrier, 3 + following + more)

    mine = pl.ds(pl.multiple_of(core * (WIDTH // 2), WIDTH // 2), WIDTH // 2)
    weight_copies = []
    share_copies = []
    for at in range(2):
        weight_copies.append(
            pltpu.make_async_remote_copy(
                src_ref=w_hbm.at[mine, of_plane(given[at])],
                dst_ref=w_far.at[at, mine],
                send_sem=weight_send.at[at],
                recv_sem=weight_recv.at[at],
                device_id=(device, ally),
                device_id_type=MESH,
            )
        )
        share_copies.append(
            pltpu.make_async_remote_copy(
                src_ref=w_far.at[at, mine],
                dst_ref=w_far.at[at, mine],
                send_sem=share_send.at[at],
                recv_sem=share_recv.at[at],
                device_id=(sibling, plane),
                device_id_type=MESH,
            )
        )
    weight_copies[1].start()
    weight_copies[0].start()

    loads[0].wait()
    loads[1].wait()

    def pool(source, rows):
        row = lax.broadcasted_iota(jnp.int32, (rows, 2 * rows), 0)
        col = lax.broadcasted_iota(jnp.int32, (rows, 2 * rows), 1)
        pairs = jnp.where((col >> 1) == row, 0.5, 0.0).astype(jnp.bfloat16)
        return jnp.dot(pairs, source, preferred_element_type=jnp.float32).astype(jnp.bfloat16)

    def pool_columns(at, carry):
        columns = pl.ds(pl.multiple_of(at * 256, 256), 256)
        for side in range(2):
            rows = kv[side, pl.ds(OWN, 2 * B), columns]
            for level in range(1, 6):
                rows = pool(rows, 512 >> level)
                pooled[side, pl.ds(POOLED[level], 512 >> level), columns] = rows
        return carry

    lax.fori_loop(0, WIDTH // 256, pool_columns, 0)

    ahead = jnp.where(first_core, sibling, jnp.minimum(device + 1, 2 * CHIPS - 1))
    tail_copy = pltpu.make_async_remote_copy(
        src_ref=kv.at[:, pl.ds(OWN + B, B)],
        dst_ref=kv.at[:, pl.ds(0, B)],
        send_sem=tail_send.at[0],
        recv_sem=tail_recv.at[0],
        device_id=(ahead, plane),
        device_id_type=MESH,
    )
    first_copy = pltpu.make_async_remote_copy(
        src_ref=pooled.at[:, pl.ds(0, B)],
        dst_ref=kv.at[:, pl.ds(level_at(1), B)],
        send_sem=tail_send.at[1],
        recv_sem=tail_recv.at[1],
        device_id=(ahead, plane),
        device_id_type=MESH,
    )

    level_copies = []
    for level in (2, 3, 4, 5):
        rows = 512 >> level
        members = 2 ** (level - 2)
        group = chip // members
        place = device - group * (2 * members)
        for member in range(members):
            target = (group + 1) * members + member
            wanted = target < CHIPS
            if level >= 3 and member < members // 2:
                wanted = wanted & (chip // 2 ** (level - 3) % 2 == 0)
            copy = pltpu.make_async_remote_copy(
                src_ref=pooled.at[:, pl.ds(POOLED[level], rows)],
                dst_ref=kv.at[:, pl.ds(pl.multiple_of(level_at(level) + place * rows, 16), rows)],
                send_sem=level_send.at[len(level_copies)],
                recv_sem=level_recv.at[level - 2],
                device_id=(2 * jnp.minimum(target, CHIPS - 1) + 1, plane),
                device_id_type=MESH,
            )
            level_copies.append((wanted, copy))

    @pl.when(first_core)
    def _():
        first_copy.start()
        tail_copy.start()

    for wanted, copy in level_copies:
        @pl.when(wanted)
        def _():
            copy.start()

    @pl.when(level_copies[0][0])
    def _():
        level_copies[0][1].wait_send()

    @pl.when(second_core & (chip < CHIPS - 1))
    def _():
        first_copy.start()
        tail_copy.start()

    def handed(index, start, rows):
        return pltpu.make_async_remote_copy(
            src_ref=kv.at[:, pl.ds(start, rows)],
            dst_ref=kv.at[:, pl.ds(start, rows)],
            send_sem=pass_send.at[index],
            recv_sem=pass_recv.at[index],
            device_id=(sibling, plane),
            device_id_type=MESH,
        )

    hand_overs = [handed(0, level_at(2), HALF)]
    for level in (3, 4, 5):
        hand_overs.append(handed(level - 2, level_at(level), B))

    def arrived(level, rows):
        whole = kv.at[:, pl.ds(level_at(level), rows)]
        pltpu.make_async_copy(whole, whole, level_recv.at[level - 2]).wait()

    for index, level in enumerate((2, 3, 4, 5)):
        if level == 2:
            @pl.when(second_core & (chip > 0))
            def _():
                arrived(2, B)
        else:
            group = chip // 2 ** (level - 2)
            second = chip // 2 ** (level - 3) % 2

            @pl.when(second_core & (group > 0) & (second == 1))
            def _():
                arrived(level, B)

            @pl.when(second_core & (group > 0) & (second == 0))
            def _():
                arrived(level, HALF)

        @pl.when(second_core)
        def _():
            hand_overs[index].start()

    loads[2].wait()

    @pl.when(device > 0)
    def _():
        first_copy.wait_recv()

    @pl.when(first_core)
    def _():
        for copy in hand_overs:
            copy.wait_recv()

    def nt(left, right):
        return lax.dot_general(
            left, right, (((1,), (1,)), ((), ())), preferred_element_type=jnp.float32
        )

    lower = lax.broadcasted_iota(jnp.int32, (HALF, HALF), 0) >= lax.broadcasted_iota(
        jnp.int32, (HALF, HALF), 1
    )

    def attend(block):
        beta = 2 * device + block
        rows = pl.ds(block * B, B)
        prior_bias = jnp.where(beta >= 1, 0.0, NEG)
        biases = []
        for level in range(1, 6):
            there = beta // 2**level >= 1
            whole = there & (beta // 2 ** (level - 1) % 2 == 1)
            biases.append(jnp.where(there, float(level), NEG))
            biases.append(jnp.where(whole, float(level), NEG))

        def one_head(head, carry):
            columns = pl.ds(pl.multiple_of(head * DH, DH), DH)
            queries = q_ref[rows, columns]
            pieces = []
            starts = [block * B, block * B + B] + [level_at(level) for level in range(1, 6)]
            for at, start in enumerate(starts):
                dots = nt(queries, kv[0, pl.ds(start, B), columns]) * SCALE
                left, right = dots[:, :HALF], dots[:, HALF:]
                if at == 0:
                    left, right = left + prior_bias, right + prior_bias
                elif at == 1:
                    left = jnp.concatenate([jnp.where(lower, left[:HALF], NEG), left[HALF:]], 0)
                    right = jnp.concatenate(
                        [jnp.full((HALF, HALF), NEG), jnp.where(lower, right[HALF:], NEG)], 0
                    )
                else:
                    left = left + biases[2 * at - 4]
                    right = right + biases[2 * at - 3]
                pieces += [left, right]
            peak = functools.reduce(jnp.maximum, pieces)
            peak = jnp.max(peak, axis=1, keepdims=True)
            total = jnp.zeros((B, HALF), jnp.float32)
            summed = jnp.zeros((B, DH), jnp.float32)
            for at, start in enumerate(starts):
                left = jnp.exp2(pieces[2 * at] - peak)
                right = jnp.exp2(pieces[2 * at + 1] - peak)
                total = total + left + right
                probs = jnp.concatenate([left, right], 1).astype(jnp.bfloat16)
                summed = summed + jnp.dot(
                    probs, kv[1, pl.ds(start, B), columns], preferred_element_type=jnp.float32
                )
            total = jnp.sum(total, axis=1, keepdims=True)
            attended[rows, columns] = (summed / total).astype(jnp.bfloat16)
            return carry

        lax.fori_loop(0, HEADS, one_head, 0)

    def block_rows(block):
        return pl.ds(block * B, B)

    far_copies = []
    sum_copies = []
    for block in range(2):
        far_copies.append(
            pltpu.make_async_remote_copy(
                src_ref=attended.at[block_rows(block)],
                dst_ref=far.at[block_rows(block)],
                send_sem=far_send.at[block],
                recv_sem=far_recv.at[block],
                device_id=(device, ally),
                device_id_type=MESH,
            )
        )
        sum_copies.append(
            pltpu.make_async_remote_copy(
                src_ref=partial.at[block_rows(block)],
                dst_ref=landed.at[block_rows(block)],
                send_sem=sum_send.at[block],
                recv_sem=sum_recv.at[block],
                device_id=(device, peer),
                device_id_type=MESH,
            )
        )

    def project(block, at):
        rows = block_rows(block)

        def tile(step, carry):
            columns = pl.ds(pl.multiple_of(step * 256, 256), 256)
            term = jnp.dot(
                attended[rows, :], w_own[at, :, columns], preferred_element_type=jnp.float32
            ) + jnp.dot(far[rows, :], w_far[at, :, columns], preferred_element_type=jnp.float32)
            if at:
                partial[rows, columns] = term.astype(jnp.bfloat16)
            else:
                own[rows, columns] = term
            return carry

        lax.fori_loop(0, WIDTH // 256, tile, 0)

    attend(1)
    far_copies[1].start()

    @pl.when(device > 0)
    def _():
        tail_copy.wait_recv()

    for at in (1, 0):
        weight_copies[at].wait_recv()
        share_copies[at].start()

    attend(0)
    far_copies[0].start()

    loads[3].wait()
    loads[4].wait()
    share_copies[1].wait_recv()
    share_copies[0].wait_recv()

    for block in (1, 0):
        far_copies[block].wait_recv()
        project(block, 1)
        sum_copies[block].start()
    for block in (1, 0):
        project(block, 0)
    for block in (1, 0):
        rows = block_rows(block)
        sum_copies[block].wait_recv()
        out_ref[rows, :] = (own[rows, :] + landed[rows, :].astype(jnp.float32)).astype(
            jnp.bfloat16
        )

    for at in range(2):
        weight_copies[at].wait_send()
        share_copies[at].wait_send()
        far_copies[at].wait_send()
        sum_copies[at].wait_send()
    for at, (wanted, copy) in enumerate(level_copies):
        if at:
            @pl.when(wanted)
            def _():
                copy.wait_send()

    @pl.when(device < 2 * CHIPS - 1)
    def _():
        first_copy.wait_send()
        tail_copy.wait_send()

    @pl.when(second_core)
    def _():
        for copy in hand_overs:
            copy.wait_send()


def per_device(query, key, value, out_weight):
    tokens = query.shape[0]
    dma = pltpu.SemaphoreType.DMA
    bf16 = jnp.bfloat16
    return pl.pallas_call(
        kernel,
        out_shape=jax.ShapeDtypeStruct((tokens, WIDTH), bf16),
        in_specs=[pl.BlockSpec(memory_space=pl.ANY)] * 4,
        out_specs=pl.BlockSpec(memory_space=pltpu.VMEM),
        scratch_shapes=[
            pltpu.VMEM((2, ROWS, WIDTH), bf16),
            pltpu.VMEM((2, 512, WIDTH), bf16),
            pltpu.VMEM((tokens, WIDTH), bf16),
            pltpu.VMEM((2, WIDTH, WIDTH), bf16),
            pltpu.VMEM((2, WIDTH, WIDTH), bf16),
            pltpu.VMEM((tokens, WIDTH), bf16),
            pltpu.VMEM((tokens, WIDTH), bf16),
            pltpu.VMEM((tokens, WIDTH), bf16),
            pltpu.VMEM((tokens, WIDTH), jnp.float32),
            pltpu.VMEM((tokens, WIDTH), bf16),
            dma((5,)),
            dma((2,)),
            dma((2,)),
            dma((15,)),
            dma((4,)),
            dma((4,)),
            dma((4,)),
            dma((2,)),
            dma((2,)),
            dma((2,)),
            dma((2,)),
            dma((2,)),
            dma((2,)),
            dma((2,)),
            dma((2,)),
        ],
        compiler_params=pltpu.CompilerParams(
            collective_id=0, has_side_effects=True, vmem_limit_bytes=56 << 20
        ),
        cost_estimate=pl.CostEstimate(
            flops=8_000_000_000, bytes_accessed=13_000_000, transcendentals=7_400_000
        ),
        name="attend_and_project",
    )(query, key, value, out_weight)


def solution(mesh):
    in_specs = (P("seq", "head"), P("seq", "head"), P("seq", "head"), P("head", None))
    out_specs = P("seq", "head")
    return jax.shard_map(
        per_device, mesh=mesh, in_specs=in_specs, out_specs=out_specs, check_vma=False
    )
```

```python
import functools
import math

import jax
import jax.numpy as jnp
from jax import lax
from jax.experimental import pallas as pl
from jax.experimental.pallas import tpu as pltpu
from jax.sharding import PartitionSpec as P

DH = 128
B = 256
HALF = 128
WIDTH = 1024
GROUPS = 2
SPAN = WIDTH // GROUPS
HEADS = SPAN // DH
SIDE = 4
CHIPS = SIDE * SIDE
PLANES = 4
CHUNK = 256
CHUNKS = 2 * B // CHUNK
NEG = -1e30
SCALE = math.log2(math.e) / math.sqrt(DH)
MESH = pl.DeviceIdType.MESH


OWN = B
ROWS = 8 * B
LEVEL = {level: (2 + level) * B for level in range(1, 6)}
POOLED = {1: 0, 2: 256, 3: 384, 4: 448, 5: 480}
SHARED = ("two_s", "3a_s", "3b_s", "4a_s", "4b_s", "5a_s", "5b_s")
COLUMN = ("four_1", "four_2", "four_3", "five_1", "five_2", "five_3")
LINKS = ("tail", "first", "two", "three_near", "three_far", "four_x", "five_near", "five_far")
LINKS += COLUMN + SHARED
ARRIVALS = ("tail", "first", "two", "three_a", "three_b", "four_x", "five_a", "five_b")
ARRIVALS += COLUMN + SHARED


def aligned(at, unit):
    return pl.multiple_of(at, unit)


def kernel(
    q_hbm,
    k_hbm,
    v_hbm,
    w_hbm,
    out_ref,
    kv,
    pooled,
    gathered_five,
    q_ref,
    w_ref,
    attended,
    far_sum,
    near_sum,
    far_landed,
    near_landed,
    own,
    load_sem,
    link_send,
    link_recv,
    far_send,
    far_recv,
    near_send,
    near_recv,
):
    device = lax.axis_index("seq")
    plane = lax.axis_index("head")
    chip = device // 2
    core = device % 2
    x = chip // SIDE
    y = chip % SIDE

    def at_chip(chip_at):
        return jnp.clip(chip_at, 0, CHIPS - 1) * 2 + core

    def in_column(step):
        return (y + step) % SIDE

    odd = y % 2 == 1
    even = y % 2 == 0
    lower_half = y < 2
    upper_half = y >= 2
    sibling = 2 * chip + 1 - core
    above = (plane + 1) % PLANES
    below = (plane + 3) % PLANES
    across = (plane + 2) % PLANES
    first_core = core == 0
    second_core = core == 1
    sees = {
        "3a": chip >= 2,
        "3b": (chip >= 2) & odd,
        "4a": x >= 1,
        "4b": (x >= 1) & upper_half,
        "5a": x >= 2,
        "5b": x == SIDE - 1,
    }

    def column_needs(step):
        return (x >= 1) & (lower_half | (in_column(step) >= 2))

    def column_gives(step):
        return (x >= 1) & (upper_half | (in_column(-step) < 2))

    def when(condition, act):
        pl.when(condition)(act)

    loads = []
    for side, source in ((0, k_hbm), (1, v_hbm)):
        for group in range(GROUPS):
            loads.append(
                pltpu.make_async_copy(
                    source.at[:, pl.ds(group * SPAN, SPAN)],
                    kv.at[group, side, pl.ds(OWN, 2 * B)],
                    load_sem.at[len(loads)],
                )
            )
    loads.append(pltpu.make_async_copy(q_hbm, q_ref, load_sem.at[len(loads)]))
    loads.append(pltpu.make_async_copy(w_hbm, w_ref, load_sem.at[len(loads)]))
    for load in loads:
        load.start()

    barrier = pltpu.get_barrier_semaphore()

    def greet(seq_at, plane_at):
        pl.semaphore_signal(barrier, inc=1, device_id=(seq_at, plane_at), device_id_type=MESH)

    greet(device, above)
    greet(device, below)
    greet(sibling, plane)
    asked = 3

    def relation(from_there, source, to_there):
        when(from_there, lambda: greet(source, plane))
        return jnp.where(to_there, 1, 0)

    asked += relation(chip > 0, at_chip(chip - 1), chip < CHIPS - 1)
    asked += relation(
        first_core & (chip > 0),
        jnp.maximum(device - 1, 0),
        second_core & (chip < CHIPS - 1),
    )
    asked += relation(x > 0, at_chip(chip - SIDE), x < SIDE - 1)
    asked += relation(chip >= 2, at_chip(chip - 2), chip + 2 < CHIPS)
    asked += relation((chip >= 3) & odd, at_chip(chip - 3), (chip + 3 < CHIPS) & even)
    for step in (1, 2, 3):
        asked += relation(
            (x < 2) | column_gives(step),
            at_chip(x * SIDE + in_column(-step)),
            (x < 2) | column_needs(step),
        )
    asked += relation(x >= 2, at_chip(y), x == 0)
    asked += relation(x == 3, at_chip(SIDE + y), x < 2)

    def pairs(rows):
        row = lax.broadcasted_iota(jnp.int32, (rows, 2 * rows), 0)
        col = lax.broadcasted_iota(jnp.int32, (rows, 2 * rows), 1)
        return jnp.where((col >> 1) == row, 0.5, 0.0).astype(jnp.bfloat16)

    def pool(half, rows):
        return jnp.dot(half, rows, preferred_element_type=jnp.float32).astype(jnp.bfloat16)

    for load in loads[: 2 * GROUPS]:
        load.wait()

    tiles = [
        (group, side, pl.ds(at, 256))
        for group in range(GROUPS)
        for side in range(2)
        for at in range(0, SPAN, 256)
    ]
    half = pairs(HALF)
    for group, side, columns in tiles:
        for quarter in range(2):
            rows = kv[group, side, pl.ds(OWN + quarter * B, B), columns]
            pooled[group, side, pl.ds(quarter * HALF, HALF), columns] = pool(half, rows)
    for level in range(2, 6):
        count_out = 512 >> level
        half = pairs(count_out)
        for group, side, columns in tiles:
            rows = pooled[group, side, pl.ds(POOLED[level - 1], 2 * count_out), columns]
            rows = pool(half, rows)
            pooled[group, side, pl.ds(POOLED[level], count_out), columns] = rows
            if level == 5:
                gathered_five[group, side, pl.ds(aligned(y * 16, 16), 16), columns] = rows

    pl.semaphore_wait(barrier, asked)

    def link(name, arrival, group, source, target, to):
        return pltpu.make_async_remote_copy(
            src_ref=source,
            dst_ref=target,
            send_sem=link_send.at[group, LINKS.index(name)],
            recv_sem=link_recv.at[group, ARRIVALS.index(arrival)],
            device_id=(to, plane),
            device_id_type=MESH,
        )

    def part(ref, group, start, rows):
        return ref.at[group, :, pl.ds(start, rows)]

    def same(name, group, ref, start, rows, to):
        piece = part(ref, group, start, rows)
        return link(name, name, group, piece, piece, to)

    def piece_at(level, half):
        return aligned(LEVEL[level] + half * HALF + core * 64, 64)

    def slot_four(at):
        return aligned(LEVEL[4] + at // 2 * HALF + core * 64 + at % 2 * 32, 32)

    def copies_of(group):
        c = {}
        to = jnp.where(first_core, sibling, jnp.minimum(device + 1, 2 * CHIPS - 1))
        tail = part(kv, group, OWN + B, B)
        c["tail"] = link("tail", "tail", group, tail, part(kv, group, 0, B), to)
        first = part(pooled, group, 0, HALF)
        c["first"] = link("first", "first", group, first, part(kv, group, LEVEL[1], HALF), to)
        two = aligned(LEVEL[2] + core * HALF, HALF)
        source = part(pooled, group, POOLED[2], HALF)
        c["two"] = link("two", "two", group, source, part(kv, group, two, HALF), at_chip(chip + 1))
        c["two_s"] = same("two_s", group, kv, two, HALF, sibling)
        three = part(pooled, group, POOLED[3], 64)
        for half, name in enumerate("ab"):
            target = part(kv, group, piece_at(3, half), 64)
            arrival = "three_" + name
            c["near_" + name] = link("three_near", arrival, group, three, target, at_chip(chip + 2))
        target = part(kv, group, piece_at(3, 0), 64)
        c["far_a"] = link("three_far", "three_a", group, three, target, at_chip(chip + 3))
        four = part(pooled, group, POOLED[4], 32)
        target = part(kv, group, slot_four(y), 32)
        c["four_x"] = link("four_x", "four_x", group, four, target, at_chip(chip + SIDE))
        slot = aligned(y * 16, 16)
        for step in (1, 2, 3):
            to = at_chip(x * SIDE + in_column(step))
            c[f"four_{step}"] = same(f"four_{step}", group, kv, slot_four(y), 32, to)
            c[f"five_{step}"] = same(f"five_{step}", group, gathered_five, slot, 16, to)
        five = gathered_five.at[group]
        first_half = part(kv, group, piece_at(5, 0), 64)
        second_half = part(kv, group, piece_at(5, 1), 64)
        c["five_03"] = link("five_near", "five_a", group, five, first_half, at_chip(12 + y))
        c["five_02"] = link("five_far", "five_a", group, five, first_half, at_chip(8 + y))
        c["five_13"] = link("five_near", "five_b", group, five, second_half, at_chip(12 + y))
        for name in sees:
            start = piece_at(int(name[0]), "ab".index(name[1]))
            c[name + "_s"] = same(name + "_s", group, kv, start, 64, sibling)
        return c

    copies = [copies_of(group) for group in range(GROUPS)]
    starts = [
        ("tail", device < 2 * CHIPS - 1),
        ("first", device < 2 * CHIPS - 1),
        ("two", chip < CHIPS - 1),
        ("near_a", even & (chip + 2 < CHIPS)),
        ("near_b", odd & (chip + 2 < CHIPS)),
        ("far_a", even & (chip + 3 < CHIPS)),
        ("four_x", x < SIDE - 1),
        ("five_03", x == 0),
        ("five_02", x == 0),
        ("five_13", x == 1),
        ("two_s", chip > 0),
    ]
    for step in (1, 2, 3):
        starts.append((f"four_{step}", column_needs(step)))
        starts.append((f"five_{step}", x < 2))
    for name in sees:
        starts.append((name + "_s", sees[name]))
    starts = dict(starts)

    def begin(group, *names):
        for name in names:
            when(starts[name], copies[group][name].start)

    def arrived(group, name, condition):
        when(condition, copies[group][name].wait_recv)

    def send_first(group):
        begin(group, "five_1", "five_3", "five_2", "four_x", "two", "near_a", "near_b", "far_a")

        @pl.when(first_core)
        def _():
            copies[group]["tail"].start()
            copies[group]["first"].start()

    def send_second(group):
        arrived(group, "four_x", x >= 1)
        begin(group, "four_1", "four_3", "four_2")
        for step in (1, 2, 3):
            arrived(group, f"five_{step}", x < 2)
        begin(group, "five_03", "five_02", "five_13")

    def send_last(group):
        begin(group, "first", "tail")

    def pass_on(group):
        arrived(group, "near_a", sees["3a"])
        arrived(group, "near_b", sees["3b"])
        begin(group, "3a_s", "3b_s")
        for step in (1, 2, 3):
            arrived(group, f"four_{step}", column_gives(step))
        begin(group, "4a_s", "4b_s")
        arrived(group, "two", chip > 0)
        begin(group, "two_s")
        arrived(group, "five_02", sees["5a"])
        arrived(group, "five_13", sees["5b"])
        begin(group, "5a_s", "5b_s")

    def ready(group):
        for name in sees:
            arrived(group, name + "_s", sees[name])
        arrived(group, "two_s", chip > 0)
        arrived(group, "first", device > 0)
        arrived(group, "tail", device > 0)
        half = pairs(HALF)
        for at, side, columns in tiles:
            if at == group:
                kv[group, side, pl.ds(LEVEL[1] + HALF, HALF), columns] = pool(
                    half, kv[group, side, pl.ds(0, B), columns]
                )

    for group in range(GROUPS):
        send_first(group)

    def clear(start, rows):
        kv[:, :, pl.ds(start, rows), :] = jnp.zeros((GROUPS, 2, rows, SPAN), jnp.bfloat16)

    @pl.when(device == 0)
    def _():
        clear(0, B)
        clear(LEVEL[1], HALF)

    @pl.when(chip == 0)
    def _():
        clear(LEVEL[2], B)

    for name in sees:
        when(
            jnp.logical_not(sees[name]),
            functools.partial(clear, LEVEL[int(name[0])] + "ab".index(name[1]) * HALF, HALF),
        )

    for group in range(GROUPS):
        send_second(group)

    @pl.when(second_core)
    def _():
        for group in range(GROUPS):
            when(starts["two"], copies[group]["two"].wait_send)
        for group in range(GROUPS):
            send_last(group)

    @pl.when(first_core)
    def _():
        for group in range(GROUPS):
            pass_on(group)

    def make_ready(group):
        when(second_core, functools.partial(pass_on, group))
        ready(group)

    loads[2 * GROUPS].wait()

    def nt(left, right):
        return lax.dot_general(
            left, right, (((1,), (1,)), ((), ())), preferred_element_type=jnp.float32
        )

    past = lax.broadcasted_iota(jnp.int32, (HALF, HALF), 0) <= lax.broadcasted_iota(
        jnp.int32, (HALF, HALF), 1
    )

    def attend(block, group):
        beta = 2 * device + block
        rows = pl.ds(block * B, B)
        prior = jnp.where(beta >= 1, 0.0, NEG)
        biases = [prior, prior, None, None]
        for level in range(1, 6):
            there = beta // 2**level >= 1
            whole = there & (beta // 2 ** (level - 1) % 2 == 1)
            biases.append(jnp.where(there, float(level), NEG))
            biases.append(jnp.where(whole, float(level), NEG))
        starts = [block * B, block * B + B] + [LEVEL[level] for level in range(1, 6)]

        def one_head(head):
            columns = pl.ds(head * DH, DH)
            own_columns = pl.ds(group * SPAN + head * DH, DH)
            queries = q_ref[rows, own_columns]
            halves = []
            peak = None
            for at, start in enumerate(starts):
                dots = nt(kv[group, 0, pl.ds(start, B), columns], queries)
                if at == 1:
                    top = jnp.concatenate(
                        [jnp.where(past, dots[:HALF, :HALF], NEG), dots[:HALF, HALF:]], 1
                    )
                    low = jnp.concatenate(
                        [jnp.full((HALF, HALF), NEG), jnp.where(past, dots[HALF:, HALF:], NEG)], 1
                    )
                else:
                    top, low = dots[:HALF], dots[HALF:]
                halves += [top, low]
            for dots, bias in zip(halves, biases):
                high = jnp.max(dots, axis=0, keepdims=True) * SCALE
                if bias is not None:
                    high = high + bias
                peak = high if peak is None else jnp.maximum(peak, high)
            total = jnp.zeros((1, B), jnp.float32)
            summed = jnp.zeros((DH, B), jnp.float32)
            for at, start in enumerate(starts):
                weights = []
                for dots, bias in zip(halves[2 * at : 2 * at + 2], biases[2 * at : 2 * at + 2]):
                    shift = peak if bias is None else peak - bias
                    weights.append(jnp.exp2(dots * SCALE - shift))
                weights = jnp.concatenate(weights, 0)
                total = total + jnp.sum(weights, axis=0, keepdims=True)
                values = jnp.transpose(kv[group, 1, pl.ds(start, B), columns])
                summed = summed + jnp.dot(
                    values, weights.astype(jnp.bfloat16), preferred_element_type=jnp.float32
                )
            attended[rows, own_columns] = jnp.transpose(summed / total).astype(jnp.bfloat16)

        for head in range(HEADS):
            one_head(head)

    def term(chunk, target, at):
        columns = pl.ds(aligned(target * WIDTH + at * 256, 256), 256)
        return jnp.dot(
            attended[pl.ds(chunk * CHUNK, CHUNK), :],
            w_ref[:, columns],
            preferred_element_type=jnp.float32,
        )

    def sends(send, recv, source, landed, chunk, way, to, at):
        rows = pl.ds(chunk * CHUNK, CHUNK)
        columns = pl.ds(at * 512, 512)
        return pltpu.make_async_remote_copy(
            src_ref=source.at[way, rows, columns],
            dst_ref=landed.at[way, rows, columns],
            send_sem=send.at[chunk, way, at],
            recv_sem=recv.at[chunk, way, at],
            device_id=(device, to),
            device_id_type=MESH,
        )

    ways = ((0, above), (1, below))
    far_copies = [
        [sends(far_send, far_recv, far_sum, far_landed, chunk, way, to, 0) for way, to in ways]
        for chunk in range(CHUNKS)
    ]
    near_copies = [
        [
            [sends(near_send, near_recv, near_sum, near_landed, chunk, way, to, at) for at in range(2)]
            for way, to in ways
        ]
        for chunk in range(CHUNKS)
    ]

    def tile(at):
        return pl.ds(at * 256, 256)

    def project_far(chunk):
        rows = pl.ds(chunk * CHUNK, CHUNK)
        for way in range(2):
            for at in range(2):
                far_sum[way, rows, tile(at)] = term(chunk, across, 2 * way + at).astype(jnp.bfloat16)
            far_copies[chunk][way].start()

    def project_near(chunk):
        rows = pl.ds(chunk * CHUNK, CHUNK)
        for way, to in ways:
            for at in range(2):
                place = 2 * (1 - way) + at
                near_sum[way, rows, tile(place)] = term(chunk, to, place).astype(jnp.bfloat16)
            near_copies[chunk][way][1 - way].start()

    def project_relay(chunk):
        rows = pl.ds(chunk * CHUNK, CHUNK)
        for way, to in ways:
            far_copies[chunk][way].wait_recv()
            for at in range(2):
                place = 2 * way + at
                near_sum[way, rows, tile(place)] = (
                    term(chunk, to, place) + far_landed[way, rows, tile(at)].astype(jnp.float32)
                ).astype(jnp.bfloat16)
            near_copies[chunk][way][way].start()

    def project_own(chunk):
        rows = pl.ds(chunk * CHUNK, CHUNK)
        for at in range(4):
            own[rows, tile(at)] = term(chunk, plane, at)

    order = (1, 0)
    for group in range(GROUPS):
        make_ready(group)
        if group < GROUPS - 1:
            for block in order:
                attend(block, group)
    loads[2 * GROUPS + 1].wait()
    for block in order:
        attend(block, GROUPS - 1)
        project_far(block)
        project_near(block)
    for chunk in order:
        project_relay(chunk)
    for chunk in order:
        project_own(chunk)
    for chunk in order:
        rows = pl.ds(chunk * CHUNK, CHUNK)
        for way in range(2):
            for at in range(2):
                near_copies[chunk][way][at].wait_recv()
        out_ref[rows, :] = (
            own[rows, :]
            + near_landed[0, rows, :].astype(jnp.float32)
            + near_landed[1, rows, :].astype(jnp.float32)
        ).astype(jnp.bfloat16)

    for chunk in order:
        for way in range(2):
            far_copies[chunk][way].wait_send()
            for at in range(2):
                near_copies[chunk][way][at].wait_send()
    for group in range(GROUPS):
        for name, condition in starts.items():
            if name == "two":
                condition = condition & first_core
            when(condition, copies[group][name].wait_send)


def per_device(query, key, value, out_weight):
    tokens = query.shape[0]
    dma = pltpu.SemaphoreType.DMA
    bf16 = jnp.bfloat16
    return pl.pallas_call(
        kernel,
        out_shape=jax.ShapeDtypeStruct((tokens, WIDTH), bf16),
        in_specs=[pl.BlockSpec(memory_space=pl.ANY)] * 4,
        out_specs=pl.BlockSpec(memory_space=pltpu.VMEM),
        scratch_shapes=[
            pltpu.VMEM((GROUPS, 2, ROWS, SPAN), bf16),
            pltpu.VMEM((GROUPS, 2, 496, SPAN), bf16),
            pltpu.VMEM((GROUPS, 2, 64, SPAN), bf16),
            pltpu.VMEM((tokens, WIDTH), bf16),
            pltpu.VMEM((WIDTH, PLANES * WIDTH), bf16),
            pltpu.VMEM((tokens, WIDTH), bf16),
            pltpu.VMEM((2, tokens, WIDTH // 2), bf16),
            pltpu.VMEM((2, tokens, WIDTH), bf16),
            pltpu.VMEM((2, tokens, WIDTH // 2), bf16),
            pltpu.VMEM((2, tokens, WIDTH), bf16),
            pltpu.VMEM((tokens, WIDTH), jnp.float32),
            dma((2 * GROUPS + 2,)),
            dma((GROUPS, len(LINKS))),
            dma((GROUPS, len(LINKS))),
            dma((CHUNKS, 2, 1)),
            dma((CHUNKS, 2, 1)),
            dma((CHUNKS, 2, 2)),
            dma((CHUNKS, 2, 2)),
        ],
        compiler_params=pltpu.CompilerParams(
            collective_id=0, has_side_effects=True, vmem_limit_bytes=56 << 20
        ),
        cost_estimate=pl.CostEstimate(
            flops=8_000_000_000, bytes_accessed=13_000_000, transcendentals=7_400_000
        ),
        name="attend_and_project",
    )(query, key, value, out_weight)


def solution(mesh):
    in_specs = (P("seq", "head"), P("seq", "head"), P("seq", "head"), P("head", None))
    out_specs = P("seq", "head")
    return jax.shard_map(
        per_device, mesh=mesh, in_specs=in_specs, out_specs=out_specs, check_vma=False
    )
```

```python
import functools
import math

import jax
import jax.numpy as jnp
from jax import lax
from jax.experimental import pallas as pl
from jax.experimental.pallas import tpu as pltpu
from jax.sharding import PartitionSpec as P

DH = 128
B = 256
HALF = 128
WIDTH = 1024
GROUPS = 2
SPAN = WIDTH // GROUPS
HEADS = SPAN // DH
SIDE = 4
CHIPS = SIDE * SIDE
PLANES = 4
CHUNK = 256
CHUNKS = 2 * B // CHUNK
NEG = -1e30
SCALE = math.log2(math.e) / math.sqrt(DH)
MESH = pl.DeviceIdType.MESH


OWN = B
ROWS = 8 * B
LEVEL = {level: (2 + level) * B for level in range(1, 6)}
POOLED = {1: 0, 2: 256, 3: 384, 4: 448, 5: 480}
SHARED = ("two_s", "3a_s", "3b_s", "4a_s", "4b_s", "5a_s", "5b_s")
COLUMN = ("four_1", "four_2", "four_3", "five_1", "five_2", "five_3")
LINKS = ("tail", "first", "two", "three_1", "three_2", "four_x", "five_near", "five_far")
LINKS += COLUMN + SHARED


def aligned(at, unit):
    return pl.multiple_of(at, unit)


def kernel(
    q_hbm,
    k_hbm,
    v_hbm,
    w_hbm,
    out_ref,
    kv,
    pooled,
    gathered_five,
    q_ref,
    w_ref,
    attended,
    far_sum,
    near_sum,
    far_landed,
    near_landed,
    own,
    load_sem,
    link_send,
    link_recv,
    far_send,
    far_recv,
    near_send,
    near_recv,
):
    device = lax.axis_index("seq")
    plane = lax.axis_index("head")
    chip = device // 2
    core = device % 2
    x = chip // SIDE
    y = chip % SIDE

    def at_chip(chip_at):
        return jnp.clip(chip_at, 0, CHIPS - 1) * 2 + core

    def in_column(step):
        return (y + step) % SIDE

    odd = y % 2 == 1
    even = y % 2 == 0
    lower_half = y < 2
    upper_half = y >= 2
    sibling = 2 * chip + 1 - core
    above = (plane + 1) % PLANES
    below = (plane + 3) % PLANES
    across = (plane + 2) % PLANES
    first_core = core == 0
    second_core = core == 1
    three_first = (y == 0) | (y == 3) | (x >= 1)
    three_second = upper_half | (x >= 1)
    five_first = (x == SIDE - 1) | (x == 0)
    sees = {
        "3a": jnp.where(odd, three_first, three_second),
        "3b": jnp.where(odd, three_second, three_first),
        "4a": x >= 1,
        "4b": (x >= 1) & upper_half,
        "5a": x >= 2,
        "5b": (x == SIDE - 1) | (x == 0),
    }

    def column_needs(step):
        return (x >= 1) & (lower_half | (in_column(step) >= 2))

    def column_gives(step):
        return (x >= 1) & (upper_half | (in_column(-step) < 2))

    def when(condition, act):
        pl.when(condition)(act)

    loads = []
    for side, source in ((0, k_hbm), (1, v_hbm)):
        for group in range(GROUPS):
            loads.append(
                pltpu.make_async_copy(
                    source.at[:, pl.ds(group * SPAN, SPAN)],
                    kv.at[group, side, pl.ds(OWN, 2 * B)],
                    load_sem.at[len(loads)],
                )
            )
    loads.append(pltpu.make_async_copy(q_hbm, q_ref, load_sem.at[len(loads)]))
    loads.append(pltpu.make_async_copy(w_hbm, w_ref, load_sem.at[len(loads)]))
    for load in loads:
        load.start()

    barrier = pltpu.get_barrier_semaphore()

    def greet(seq_at, plane_at):
        pl.semaphore_signal(barrier, inc=1, device_id=(seq_at, plane_at), device_id_type=MESH)

    greet(device, above)
    greet(device, below)
    greet(sibling, plane)
    asked = 3

    def relation(from_there, source, to_there):
        when(from_there, lambda: greet(source, plane))
        return jnp.where(to_there, 1, 0)

    asked += relation(chip > 0, at_chip(chip - 1), chip < CHIPS - 1)
    asked += relation(
        first_core & (chip > 0),
        jnp.maximum(device - 1, 0),
        second_core & (chip < CHIPS - 1),
    )
    asked += relation(x > 0, at_chip(chip - SIDE), x < SIDE - 1)
    down = at_chip(x * SIDE + in_column(-1))
    three_to = at_chip(chip - 1 + jnp.where(upper_half, SIDE, jnp.where(y == 0, SIDE, 0)))
    three_from = at_chip(x * SIDE + in_column(1) - jnp.where((y == 1) | (y == 2), SIDE, 0))
    asked += relation(three_first, three_from, lower_half | (x < SIDE - 1))
    asked += relation(three_second, at_chip(x * SIDE + in_column(1)), three_first)
    for step in (1, 2, 3):
        asked += relation(
            (x < 2) | column_gives(step),
            at_chip(x * SIDE + in_column(-step)),
            (x < 2) | column_needs(step),
        )
    x_down = at_chip((x + 3) % SIDE * SIDE + y)
    asked += relation(x != 1, at_chip((x + 1) % SIDE * SIDE + y), x != 2)

    def pairs(rows):
        row = lax.broadcasted_iota(jnp.int32, (rows, 2 * rows), 0)
        col = lax.broadcasted_iota(jnp.int32, (rows, 2 * rows), 1)
        return jnp.where((col >> 1) == row, 0.5, 0.0).astype(jnp.bfloat16)

    def pool(half, rows):
        return jnp.dot(half, rows, preferred_element_type=jnp.float32).astype(jnp.bfloat16)

    for load in loads[: 2 * GROUPS]:
        load.wait()

    tiles = [
        (group, side, pl.ds(at, 256))
        for group in range(GROUPS)
        for side in range(2)
        for at in range(0, SPAN, 256)
    ]
    half = pairs(HALF)
    for group, side, columns in tiles:
        for quarter in range(2):
            rows = kv[group, side, pl.ds(OWN + quarter * B, B), columns]
            pooled[group, side, pl.ds(quarter * HALF, HALF), columns] = pool(half, rows)
    for level in range(2, 6):
        count_out = 512 >> level
        half = pairs(count_out)
        for group, side, columns in tiles:
            rows = pooled[group, side, pl.ds(POOLED[level - 1], 2 * count_out), columns]
            rows = pool(half, rows)
            pooled[group, side, pl.ds(POOLED[level], count_out), columns] = rows
            if level == 5:
                gathered_five[group, side, pl.ds(aligned(y * 16, 16), 16), columns] = rows

    pl.semaphore_wait(barrier, asked)

    def link(name, group, source, target, to):
        return pltpu.make_async_remote_copy(
            src_ref=source,
            dst_ref=target,
            send_sem=link_send.at[group, LINKS.index(name)],
            recv_sem=link_recv.at[group, LINKS.index(name)],
            device_id=(to, plane),
            device_id_type=MESH,
        )

    def part(ref, group, start, rows):
        return ref.at[group, :, pl.ds(start, rows)]

    def same(name, group, ref, start, rows, to):
        piece = part(ref, group, start, rows)
        return link(name, group, piece, piece, to)

    def piece_at(level, half):
        return aligned(LEVEL[level] + half * HALF + core * 64, 64)

    def slot_four(at):
        return aligned(LEVEL[4] + at // 2 * HALF + core * 64 + at % 2 * 32, 32)

    def copies_of(group):
        c = {}
        to = jnp.where(first_core, sibling, jnp.minimum(device + 1, 2 * CHIPS - 1))
        tail = part(kv, group, OWN + B, B)
        c["tail"] = link("tail", group, tail, part(kv, group, 0, B), to)
        first = part(pooled, group, 0, HALF)
        c["first"] = link("first", group, first, part(kv, group, LEVEL[1], HALF), to)
        two = aligned(LEVEL[2] + core * HALF, HALF)
        source = part(pooled, group, POOLED[2], HALF)
        c["two"] = link("two", group, source, part(kv, group, two, HALF), at_chip(chip + 1))
        c["two_s"] = same("two_s", group, kv, two, HALF, sibling)
        three = part(pooled, group, POOLED[3], 64)
        target = part(kv, group, piece_at(3, y % 2), 64)
        c["three_1"] = link("three_1", group, three, target, three_to)
        c["three_2"] = same("three_2", group, kv, piece_at(3, 1 - y % 2), 64, down)
        four = part(pooled, group, POOLED[4], 32)
        target = part(kv, group, slot_four(y), 32)
        c["four_x"] = link("four_x", group, four, target, at_chip(chip + SIDE))
        slot = aligned(y * 16, 16)
        for step in (1, 2, 3):
            to = at_chip(x * SIDE + in_column(step))
            c[f"four_{step}"] = same(f"four_{step}", group, kv, slot_four(y), 32, to)
            c[f"five_{step}"] = same(f"five_{step}", group, gathered_five, slot, 16, to)
        target = part(kv, group, piece_at(5, jnp.where(x == 0, 0, 1)), 64)
        c["five_near"] = link("five_near", group, gathered_five.at[group], target, x_down)
        start = piece_at(5, jnp.where(x == 0, 1, 0))
        c["five_far"] = same("five_far", group, kv, start, 64, x_down)
        for name in sees:
            start = piece_at(int(name[0]), "ab".index(name[1]))
            c[name + "_s"] = same(name + "_s", group, kv, start, 64, sibling)
        return c

    copies = [copies_of(group) for group in range(GROUPS)]
    starts = [
        ("tail", device < 2 * CHIPS - 1),
        ("first", device < 2 * CHIPS - 1),
        ("two", chip < CHIPS - 1),
        ("three_1", lower_half | (x < SIDE - 1)),
        ("three_2", three_first),
        ("four_x", x < SIDE - 1),
        ("five_near", x < 2),
        ("five_far", five_first),
        ("two_s", chip > 0),
    ]
    for step in (1, 2, 3):
        starts.append((f"four_{step}", column_needs(step)))
        starts.append((f"five_{step}", x < 2))
    for name in sees:
        starts.append((name + "_s", sees[name]))
    starts = dict(starts)

    def begin(group, *names):
        for name in names:
            when(starts[name], copies[group][name].start)

    def arrived(group, name, condition):
        when(condition, copies[group][name].wait_recv)

    every = range(GROUPS)

    def send_first():
        for group in every:
            begin(group, "five_1", "five_3", "five_2", "four_x")
        for group in every:
            begin(group, "three_1")
        for group in every:
            begin(group, "two")

        @pl.when(first_core)
        def _():
            for group in every:
                copies[group]["tail"].start()
                copies[group]["first"].start()

    def send_second():
        for group in every:
            for step in (1, 2, 3):
                arrived(group, f"five_{step}", x < 2)
            begin(group, "five_near")
        for group in every:
            arrived(group, "four_x", x >= 1)
            begin(group, "four_1", "four_3", "four_2")
        for group in every:
            arrived(group, "three_1", three_first)
            begin(group, "three_2")
        for group in every:
            arrived(group, "five_near", five_first)
            begin(group, "five_far")

    def send_last(group):
        begin(group, "first", "tail")

    def pass_on(group):
        arrived(group, "three_2", three_second)
        begin(group, "3a_s", "3b_s")
        for step in (1, 2, 3):
            arrived(group, f"four_{step}", column_gives(step))
        begin(group, "4a_s", "4b_s")
        arrived(group, "two", chip > 0)
        begin(group, "two_s")
        arrived(group, "five_far", x >= 2)
        begin(group, "5a_s", "5b_s")

    def ready(group):
        for name in sees:
            arrived(group, name + "_s", sees[name])
        arrived(group, "two_s", chip > 0)
        arrived(group, "first", (device > 0))
        arrived(group, "tail", (device > 0))
        half = pairs(HALF)
        for at, side, columns in tiles:
            if at == group:
                kv[group, side, pl.ds(LEVEL[1] + HALF, HALF), columns] = pool(
                    half, kv[group, side, pl.ds(0, B), columns]
                )

    send_first()

    def clear(start, rows):
        kv[:, :, pl.ds(start, rows), :] = jnp.zeros((GROUPS, 2, rows, SPAN), jnp.bfloat16)

    @pl.when(device == 0)
    def _():
        clear(0, B)
        clear(LEVEL[1], HALF)

    @pl.when(chip == 0)
    def _():
        clear(LEVEL[2], B)

    for name in sees:
        when(
            jnp.logical_not(sees[name]),
            functools.partial(clear, LEVEL[int(name[0])] + "ab".index(name[1]) * HALF, HALF),
        )

    send_second()

    @pl.when(second_core)
    def _():
        for group in range(GROUPS):
            when(starts["two"], copies[group]["two"].wait_send)
        for group in range(GROUPS):
            send_last(group)

    @pl.when(first_core)
    def _():
        for group in range(GROUPS):
            pass_on(group)

    def make_ready(group):
        when(second_core, functools.partial(pass_on, group))
        ready(group)

    loads[2 * GROUPS].wait()

    def nt(left, right):
        return lax.dot_general(
            left, right, (((1,), (1,)), ((), ())), preferred_element_type=jnp.float32
        )

    past = lax.broadcasted_iota(jnp.int32, (HALF, HALF), 0) <= lax.broadcasted_iota(
        jnp.int32, (HALF, HALF), 1
    )

    def attend(block, group):
        beta = 2 * device + block
        rows = pl.ds(block * B, B)
        prior = jnp.where(beta >= 1, 0.0, NEG)
        biases = [prior, prior, None, None]
        for level in range(1, 6):
            there = beta // 2**level >= 1
            whole = there & (beta // 2 ** (level - 1) % 2 == 1)
            biases.append(jnp.where(there, float(level), NEG))
            biases.append(jnp.where(whole, float(level), NEG))
        starts = [block * B, block * B + B] + [LEVEL[level] for level in range(1, 6)]

        def one_head(head):
            columns = pl.ds(head * DH, DH)
            own_columns = pl.ds(group * SPAN + head * DH, DH)
            queries = q_ref[rows, own_columns]
            halves = []
            peak = None
            for at, start in enumerate(starts):
                dots = nt(kv[group, 0, pl.ds(start, B), columns], queries)
                if at == 1:
                    top = jnp.concatenate(
                        [jnp.where(past, dots[:HALF, :HALF], NEG), dots[:HALF, HALF:]], 1
                    )
                    low = jnp.concatenate(
                        [jnp.full((HALF, HALF), NEG), jnp.where(past, dots[HALF:, HALF:], NEG)], 1
                    )
                else:
                    top, low = dots[:HALF], dots[HALF:]
                halves += [top, low]
            for dots, bias in zip(halves, biases):
                high = jnp.max(dots, axis=0, keepdims=True) * SCALE
                if bias is not None:
                    high = high + bias
                peak = high if peak is None else jnp.maximum(peak, high)
            total = jnp.zeros((1, B), jnp.float32)
            summed = jnp.zeros((DH, B), jnp.float32)
            for at, start in enumerate(starts):
                weights = []
                for dots, bias in zip(halves[2 * at : 2 * at + 2], biases[2 * at : 2 * at + 2]):
                    shift = peak if bias is None else peak - bias
                    weights.append(jnp.exp2(dots * SCALE - shift))
                weights = jnp.concatenate(weights, 0)
                total = total + jnp.sum(weights, axis=0, keepdims=True)
                values = jnp.transpose(kv[group, 1, pl.ds(start, B), columns])
                summed = summed + jnp.dot(
                    values, weights.astype(jnp.bfloat16), preferred_element_type=jnp.float32
                )
            attended[rows, own_columns] = jnp.transpose(summed / total).astype(jnp.bfloat16)

        for head in range(HEADS):
            one_head(head)

    def term(chunk, target, at):
        columns = pl.ds(aligned(target * WIDTH + at * 256, 256), 256)
        return jnp.dot(
            attended[pl.ds(chunk * CHUNK, CHUNK), :],
            w_ref[:, columns],
            preferred_element_type=jnp.float32,
        )

    def sends(send, recv, source, landed, chunk, way, to, at):
        rows = pl.ds(chunk * CHUNK, CHUNK)
        columns = pl.ds(at * 512, 512)
        return pltpu.make_async_remote_copy(
            src_ref=source.at[way, rows, columns],
            dst_ref=landed.at[way, rows, columns],
            send_sem=send.at[chunk, way, at],
            recv_sem=recv.at[chunk, way, at],
            device_id=(device, to),
            device_id_type=MESH,
        )

    ways = ((0, above), (1, below))
    far_copies = [
        [sends(far_send, far_recv, far_sum, far_landed, chunk, way, to, 0) for way, to in ways]
        for chunk in range(CHUNKS)
    ]
    near_copies = [
        [
            [sends(near_send, near_recv, near_sum, near_landed, chunk, way, to, at) for at in range(2)]
            for way, to in ways
        ]
        for chunk in range(CHUNKS)
    ]

    def tile(at):
        return pl.ds(at * 256, 256)

    def project_far(chunk):
        rows = pl.ds(chunk * CHUNK, CHUNK)
        for way in range(2):
            for at in range(2):
                far_sum[way, rows, tile(at)] = term(chunk, across, 2 * way + at).astype(jnp.bfloat16)
            far_copies[chunk][way].start()

    def project_near(chunk):
        rows = pl.ds(chunk * CHUNK, CHUNK)
        for way, to in ways:
            for at in range(2):
                place = 2 * (1 - way) + at
                near_sum[way, rows, tile(place)] = term(chunk, to, place).astype(jnp.bfloat16)
            near_copies[chunk][way][1 - way].start()

    def project_relay(chunk):
        rows = pl.ds(chunk * CHUNK, CHUNK)
        for way, to in ways:
            far_copies[chunk][way].wait_recv()
            for at in range(2):
                place = 2 * way + at
                near_sum[way, rows, tile(place)] = (
                    term(chunk, to, place) + far_landed[way, rows, tile(at)].astype(jnp.float32)
                ).astype(jnp.bfloat16)
            near_copies[chunk][way][way].start()

    def project_own(chunk):
        rows = pl.ds(chunk * CHUNK, CHUNK)
        for at in range(4):
            own[rows, tile(at)] = term(chunk, plane, at)

    order = (1, 0)
    for group in range(GROUPS):
        make_ready(group)
        if group < GROUPS - 1:
            for block in order:
                attend(block, group)
    loads[2 * GROUPS + 1].wait()
    for block in order:
        attend(block, GROUPS - 1)
        project_far(block)
        project_near(block)
    for chunk in order:
        project_relay(chunk)
    for chunk in order:
        project_own(chunk)
    for chunk in order:
        rows = pl.ds(chunk * CHUNK, CHUNK)
        for way in range(2):
            for at in range(2):
                near_copies[chunk][way][at].wait_recv()
        out_ref[rows, :] = (
            own[rows, :]
            + near_landed[0, rows, :].astype(jnp.float32)
            + near_landed[1, rows, :].astype(jnp.float32)
        ).astype(jnp.bfloat16)

    for chunk in order:
        for way in range(2):
            far_copies[chunk][way].wait_send()
            for at in range(2):
                near_copies[chunk][way][at].wait_send()
    for group in range(GROUPS):
        for name, condition in starts.items():
            if name == "two":
                condition = condition & first_core
            when(condition, copies[group][name].wait_send)


def per_device(query, key, value, out_weight):
    tokens = query.shape[0]
    dma = pltpu.SemaphoreType.DMA
    bf16 = jnp.bfloat16
    return pl.pallas_call(
        kernel,
        out_shape=jax.ShapeDtypeStruct((tokens, WIDTH), bf16),
        in_specs=[pl.BlockSpec(memory_space=pl.ANY)] * 4,
        out_specs=pl.BlockSpec(memory_space=pltpu.VMEM),
        scratch_shapes=[
            pltpu.VMEM((GROUPS, 2, ROWS, SPAN), bf16),
            pltpu.VMEM((GROUPS, 2, 496, SPAN), bf16),
            pltpu.VMEM((GROUPS, 2, 64, SPAN), bf16),
            pltpu.VMEM((tokens, WIDTH), bf16),
            pltpu.VMEM((WIDTH, PLANES * WIDTH), bf16),
            pltpu.VMEM((tokens, WIDTH), bf16),
            pltpu.VMEM((2, tokens, WIDTH // 2), bf16),
            pltpu.VMEM((2, tokens, WIDTH), bf16),
            pltpu.VMEM((2, tokens, WIDTH // 2), bf16),
            pltpu.VMEM((2, tokens, WIDTH), bf16),
            pltpu.VMEM((tokens, WIDTH), jnp.float32),
            dma((2 * GROUPS + 2,)),
            dma((GROUPS, len(LINKS))),
            dma((GROUPS, len(LINKS))),
            dma((CHUNKS, 2, 1)),
            dma((CHUNKS, 2, 1)),
            dma((CHUNKS, 2, 2)),
            dma((CHUNKS, 2, 2)),
        ],
        compiler_params=pltpu.CompilerParams(
            collective_id=0, has_side_effects=True, vmem_limit_bytes=56 << 20
        ),
        cost_estimate=pl.CostEstimate(
            flops=8_000_000_000, bytes_accessed=13_000_000, transcendentals=7_400_000
        ),
        name="attend_and_project",
    )(query, key, value, out_weight)


def solution(mesh):
    in_specs = (P("seq", "head"), P("seq", "head"), P("seq", "head"), P("head", None))
    out_specs = P("seq", "head")
    return jax.shard_map(
        per_device, mesh=mesh, in_specs=in_specs, out_specs=out_specs, check_vma=False
    )
```

```python
import functools
import math

import jax
import jax.numpy as jnp
from jax import lax
from jax.experimental import pallas as pl
from jax.experimental.pallas import tpu as pltpu
from jax.sharding import PartitionSpec as P

DH = 128
B = 256
HALF = 128
WIDTH = 1024
GROUPS = 2
SPAN = WIDTH // GROUPS
HEADS = SPAN // DH
SIDE = 4
CHIPS = SIDE * SIDE
PLANES = 4
CHUNK = 256
CHUNKS = 2 * B // CHUNK
NEG = -1e30
SCALE = math.log2(math.e) / math.sqrt(DH)
MESH = pl.DeviceIdType.MESH


OWN = B
ROWS = 8 * B
LEVEL = {level: (2 + level) * B for level in range(1, 6)}
POOLED = {1: 0, 2: 256, 3: 384, 4: 448, 5: 480}
SHARED = ("two_s", "3a_s", "3b_s", "4a_s", "4b_s", "5a_s", "5b_s")
COLUMN = ("four_1", "four_2", "four_3", "five_1", "five_2", "five_3")
LINKS = ("tail", "first", "two", "three_1", "three_2", "four_x", "five_near", "five_far")
LINKS += COLUMN + SHARED


def aligned(at, unit):
    return pl.multiple_of(at, unit)


def kernel(
    q_hbm,
    k_hbm,
    v_hbm,
    w_hbm,
    out_ref,
    kv,
    pooled,
    gathered_five,
    q_ref,
    w_ref,
    attended,
    far_sum,
    near_sum,
    far_landed,
    near_landed,
    own,
    load_sem,
    link_send,
    link_recv,
    far_send,
    far_recv,
    near_send,
    near_recv,
):
    device = lax.axis_index("seq")
    plane = lax.axis_index("head")
    chip = device // 2
    core = device % 2
    x = chip // SIDE
    y = chip % SIDE

    def at_chip(chip_at):
        return jnp.clip(chip_at, 0, CHIPS - 1) * 2 + core

    def in_column(step):
        return (y + step) % SIDE

    odd = y % 2 == 1
    even = y % 2 == 0
    lower_half = y < 2
    upper_half = y >= 2
    sibling = 2 * chip + 1 - core
    above = (plane + 1) % PLANES
    below = (plane + 3) % PLANES
    across = (plane + 2) % PLANES
    first_core = core == 0
    second_core = core == 1
    three_first = (y == 0) | (y == 3) | (x >= 1)
    three_second = upper_half | (x >= 1)
    five_first = (x == SIDE - 1) | (x == 0)
    sees = {
        "3a": jnp.where(odd, three_first, three_second),
        "3b": jnp.where(odd, three_second, three_first),
        "4a": x >= 1,
        "4b": (x >= 1) & upper_half,
        "5a": x >= 2,
        "5b": (x == SIDE - 1) | (x == 0),
    }

    def column_needs(step):
        return (x >= 1) & (lower_half | (in_column(step) >= 2))

    def column_gives(step):
        return (x >= 1) & (upper_half | (in_column(-step) < 2))

    def when(condition, act):
        pl.when(condition)(act)

    loads = []
    for side, source in ((0, k_hbm), (1, v_hbm)):
        for group in range(GROUPS):
            loads.append(
                pltpu.make_async_copy(
                    source.at[:, pl.ds(group * SPAN, SPAN)],
                    kv.at[group, side, pl.ds(OWN, 2 * B)],
                    load_sem.at[len(loads)],
                )
            )
    loads.append(pltpu.make_async_copy(q_hbm, q_ref, load_sem.at[len(loads)]))
    loads.append(pltpu.make_async_copy(w_hbm, w_ref, load_sem.at[len(loads)]))
    for load in loads[: 2 * GROUPS]:
        load.start()

    barrier = pltpu.get_barrier_semaphore()

    def greet(seq_at, plane_at):
        pl.semaphore_signal(barrier, inc=1, device_id=(seq_at, plane_at), device_id_type=MESH)

    greet(device, above)
    greet(device, below)
    greet(sibling, plane)
    asked = 3

    def relation(from_there, source, to_there):
        when(from_there, lambda: greet(source, plane))
        return jnp.where(to_there, 1, 0)

    asked += relation(chip > 0, at_chip(chip - 1), chip < CHIPS - 1)
    asked += relation(
        first_core & (chip > 0),
        jnp.maximum(device - 1, 0),
        second_core & (chip < CHIPS - 1),
    )
    asked += relation(x > 0, at_chip(chip - SIDE), x < SIDE - 1)
    down = at_chip(x * SIDE + in_column(-1))
    three_to = at_chip(chip - 1 + jnp.where(upper_half, SIDE, jnp.where(y == 0, SIDE, 0)))
    three_from = at_chip(x * SIDE + in_column(1) - jnp.where((y == 1) | (y == 2), SIDE, 0))
    asked += relation(three_first, three_from, lower_half | (x < SIDE - 1))
    asked += relation(three_second, at_chip(x * SIDE + in_column(1)), three_first)
    for step in (1, 2, 3):
        asked += relation(
            (x < 2) | column_gives(step),
            at_chip(x * SIDE + in_column(-step)),
            (x < 2) | column_needs(step),
        )
    x_down = at_chip((x + 3) % SIDE * SIDE + y)
    asked += relation(x != 1, at_chip((x + 1) % SIDE * SIDE + y), x != 2)

    def pairs(rows):
        row = lax.broadcasted_iota(jnp.int32, (rows, 2 * rows), 0)
        col = lax.broadcasted_iota(jnp.int32, (rows, 2 * rows), 1)
        return jnp.where((col >> 1) == row, 0.5, 0.0).astype(jnp.bfloat16)

    def pool(half, rows):
        return jnp.dot(half, rows, preferred_element_type=jnp.float32).astype(jnp.bfloat16)

    for load in loads[: 2 * GROUPS]:
        load.wait()
    for load in loads[2 * GROUPS :]:
        load.start()

    tiles = [
        (group, side, pl.ds(at, 256))
        for group in range(GROUPS)
        for side in range(2)
        for at in range(0, SPAN, 256)
    ]
    half = pairs(HALF)
    for group, side, columns in tiles:
        for quarter in range(2):
            rows = kv[group, side, pl.ds(OWN + quarter * B, B), columns]
            pooled[group, side, pl.ds(quarter * HALF, HALF), columns] = pool(half, rows)
    for level in range(2, 6):
        count_out = 512 >> level
        half = pairs(count_out)
        for group, side, columns in tiles:
            rows = pooled[group, side, pl.ds(POOLED[level - 1], 2 * count_out), columns]
            rows = pool(half, rows)
            pooled[group, side, pl.ds(POOLED[level], count_out), columns] = rows
            if level == 5:
                gathered_five[group, side, pl.ds(aligned(y * 16, 16), 16), columns] = rows

    pl.semaphore_wait(barrier, asked)

    def link(name, group, source, target, to):
        return pltpu.make_async_remote_copy(
            src_ref=source,
            dst_ref=target,
            send_sem=link_send.at[group, LINKS.index(name)],
            recv_sem=link_recv.at[group, LINKS.index(name)],
            device_id=(to, plane),
            device_id_type=MESH,
        )

    def part(ref, group, start, rows):
        return ref.at[group, :, pl.ds(start, rows)]

    def same(name, group, ref, start, rows, to):
        piece = part(ref, group, start, rows)
        return link(name, group, piece, piece, to)

    def piece_at(level, half):
        return aligned(LEVEL[level] + half * HALF + core * 64, 64)

    def slot_four(at):
        return aligned(LEVEL[4] + at // 2 * HALF + core * 64 + at % 2 * 32, 32)

    def copies_of(group):
        c = {}
        to = jnp.where(first_core, sibling, jnp.minimum(device + 1, 2 * CHIPS - 1))
        tail = part(kv, group, OWN + B, B)
        c["tail"] = link("tail", group, tail, part(kv, group, 0, B), to)
        first = part(pooled, group, 0, HALF)
        c["first"] = link("first", group, first, part(kv, group, LEVEL[1], HALF), to)
        two = aligned(LEVEL[2] + core * HALF, HALF)
        source = part(pooled, group, POOLED[2], HALF)
        c["two"] = link("two", group, source, part(kv, group, two, HALF), at_chip(chip + 1))
        c["two_s"] = same("two_s", group, kv, two, HALF, sibling)
        three = part(pooled, group, POOLED[3], 64)
        target = part(kv, group, piece_at(3, y % 2), 64)
        c["three_1"] = link("three_1", group, three, target, three_to)
        c["three_2"] = same("three_2", group, kv, piece_at(3, 1 - y % 2), 64, down)
        four = part(pooled, group, POOLED[4], 32)
        target = part(kv, group, slot_four(y), 32)
        c["four_x"] = link("four_x", group, four, target, at_chip(chip + SIDE))
        slot = aligned(y * 16, 16)
        for step in (1, 2, 3):
            to = at_chip(x * SIDE + in_column(step))
            c[f"four_{step}"] = same(f"four_{step}", group, kv, slot_four(y), 32, to)
            c[f"five_{step}"] = same(f"five_{step}", group, gathered_five, slot, 16, to)
        target = part(kv, group, piece_at(5, jnp.where(x == 0, 0, 1)), 64)
        c["five_near"] = link("five_near", group, gathered_five.at[group], target, x_down)
        start = piece_at(5, jnp.where(x == 0, 1, 0))
        c["five_far"] = same("five_far", group, kv, start, 64, x_down)
        for name in sees:
            start = piece_at(int(name[0]), "ab".index(name[1]))
            c[name + "_s"] = same(name + "_s", group, kv, start, 64, sibling)
        return c

    copies = [copies_of(group) for group in range(GROUPS)]
    starts = [
        ("tail", device < 2 * CHIPS - 1),
        ("first", device < 2 * CHIPS - 1),
        ("two", chip < CHIPS - 1),
        ("three_1", lower_half | (x < SIDE - 1)),
        ("three_2", three_first),
        ("four_x", x < SIDE - 1),
        ("five_near", x < 2),
        ("five_far", five_first),
        ("two_s", chip > 0),
    ]
    for step in (1, 2, 3):
        starts.append((f"four_{step}", column_needs(step)))
        starts.append((f"five_{step}", x < 2))
    for name in sees:
        starts.append((name + "_s", sees[name]))
    starts = dict(starts)

    def begin(group, *names):
        for name in names:
            when(starts[name], copies[group][name].start)

    def arrived(group, name, condition):
        when(condition, copies[group][name].wait_recv)

    every = range(GROUPS)

    def send_first():
        for group in every:
            begin(group, "five_1", "five_3", "five_2", "four_x")
        for group in every:
            begin(group, "three_1")
        for group in every:
            begin(group, "two")

        @pl.when(first_core)
        def _():
            for group in every:
                copies[group]["tail"].start()
                copies[group]["first"].start()

    def send_second():
        for group in every:
            for step in (1, 2, 3):
                arrived(group, f"five_{step}", x < 2)
            begin(group, "five_near")
        for group in every:
            arrived(group, "four_x", x >= 1)
            begin(group, "four_1", "four_3", "four_2")
        for group in every:
            arrived(group, "three_1", three_first)
            begin(group, "three_2")
        for group in every:
            arrived(group, "five_near", five_first)
            begin(group, "five_far")

    def send_last(group):
        begin(group, "first", "tail")

    def pass_on(group):
        arrived(group, "three_2", three_second)
        begin(group, "3a_s", "3b_s")
        for step in (1, 2, 3):
            arrived(group, f"four_{step}", column_gives(step))
        begin(group, "4a_s", "4b_s")
        arrived(group, "two", chip > 0)
        begin(group, "two_s")
        arrived(group, "five_far", x >= 2)
        begin(group, "5a_s", "5b_s")

    def ready(group):
        for name in sees:
            arrived(group, name + "_s", sees[name])
        arrived(group, "two_s", chip > 0)
        arrived(group, "first", (device > 0))
        arrived(group, "tail", (device > 0))
        half = pairs(HALF)
        for at, side, columns in tiles:
            if at == group:
                kv[group, side, pl.ds(LEVEL[1] + HALF, HALF), columns] = pool(
                    half, kv[group, side, pl.ds(0, B), columns]
                )

    send_first()

    def clear(start, rows):
        kv[:, :, pl.ds(start, rows), :] = jnp.zeros((GROUPS, 2, rows, SPAN), jnp.bfloat16)

    @pl.when(device == 0)
    def _():
        clear(0, B)
        clear(LEVEL[1], HALF)

    @pl.when(chip == 0)
    def _():
        clear(LEVEL[2], B)

    for name in sees:
        when(
            jnp.logical_not(sees[name]),
            functools.partial(clear, LEVEL[int(name[0])] + "ab".index(name[1]) * HALF, HALF),
        )

    send_second()

    @pl.when(second_core)
    def _():
        for group in range(GROUPS):
            when(starts["two"], copies[group]["two"].wait_send)
        for group in range(GROUPS):
            send_last(group)

    @pl.when(first_core)
    def _():
        for group in range(GROUPS):
            pass_on(group)

    def make_ready(group):
        when(second_core, functools.partial(pass_on, group))
        ready(group)

    loads[2 * GROUPS].wait()

    def nt(left, right):
        return lax.dot_general(
            left, right, (((1,), (1,)), ((), ())), preferred_element_type=jnp.float32
        )

    past = lax.broadcasted_iota(jnp.int32, (HALF, HALF), 0) <= lax.broadcasted_iota(
        jnp.int32, (HALF, HALF), 1
    )

    def attend(block, group):
        beta = 2 * device + block
        rows = pl.ds(block * B, B)
        prior = jnp.where(beta >= 1, 0.0, NEG)
        biases = [prior, prior, None, None]
        for level in range(1, 6):
            there = beta // 2**level >= 1
            whole = there & (beta // 2 ** (level - 1) % 2 == 1)
            biases.append(jnp.where(there, float(level), NEG))
            biases.append(jnp.where(whole, float(level), NEG))
        starts = [block * B, block * B + B] + [LEVEL[level] for level in range(1, 6)]

        def one_head(head):
            columns = pl.ds(head * DH, DH)
            own_columns = pl.ds(group * SPAN + head * DH, DH)
            queries = q_ref[rows, own_columns]
            halves = []
            peak = None
            for at, start in enumerate(starts):
                dots = nt(kv[group, 0, pl.ds(start, B), columns], queries)
                if at == 1:
                    top = jnp.concatenate(
                        [jnp.where(past, dots[:HALF, :HALF], NEG), dots[:HALF, HALF:]], 1
                    )
                    low = jnp.concatenate(
                        [jnp.full((HALF, HALF), NEG), jnp.where(past, dots[HALF:, HALF:], NEG)], 1
                    )
                else:
                    top, low = dots[:HALF], dots[HALF:]
                halves += [top, low]
            for dots, bias in zip(halves, biases):
                high = jnp.max(dots, axis=0, keepdims=True) * SCALE
                if bias is not None:
                    high = high + bias
                peak = high if peak is None else jnp.maximum(peak, high)
            total = jnp.zeros((1, B), jnp.float32)
            summed = jnp.zeros((DH, B), jnp.float32)
            for at, start in enumerate(starts):
                weights = []
                for dots, bias in zip(halves[2 * at : 2 * at + 2], biases[2 * at : 2 * at + 2]):
                    shift = peak if bias is None else peak - bias
                    weights.append(jnp.exp2(dots * SCALE - shift))
                weights = jnp.concatenate(weights, 0)
                total = total + jnp.sum(weights, axis=0, keepdims=True)
                values = jnp.transpose(kv[group, 1, pl.ds(start, B), columns])
                summed = summed + jnp.dot(
                    values, weights.astype(jnp.bfloat16), preferred_element_type=jnp.float32
                )
            attended[rows, own_columns] = jnp.transpose(summed / total).astype(jnp.bfloat16)

        for head in range(HEADS):
            one_head(head)

    def term(chunk, target, at):
        columns = pl.ds(aligned(target * WIDTH + at * 256, 256), 256)
        return jnp.dot(
            attended[pl.ds(chunk * CHUNK, CHUNK), :],
            w_ref[:, columns],
            preferred_element_type=jnp.float32,
        )

    def sends(send, recv, source, landed, chunk, way, to, at):
        rows = pl.ds(chunk * CHUNK, CHUNK)
        columns = pl.ds(at * 512, 512)
        return pltpu.make_async_remote_copy(
            src_ref=source.at[way, rows, columns],
            dst_ref=landed.at[way, rows, columns],
            send_sem=send.at[chunk, way, at],
            recv_sem=recv.at[chunk, way, at],
            device_id=(device, to),
            device_id_type=MESH,
        )

    ways = ((0, above), (1, below))
    far_copies = [
        [sends(far_send, far_recv, far_sum, far_landed, chunk, way, to, 0) for way, to in ways]
        for chunk in range(CHUNKS)
    ]
    near_copies = [
        [
            [sends(near_send, near_recv, near_sum, near_landed, chunk, way, to, at) for at in range(2)]
            for way, to in ways
        ]
        for chunk in range(CHUNKS)
    ]

    def tile(at):
        return pl.ds(at * 256, 256)

    def project_far(chunk):
        rows = pl.ds(chunk * CHUNK, CHUNK)
        for way in range(2):
            for at in range(2):
                far_sum[way, rows, tile(at)] = term(chunk, across, 2 * way + at).astype(jnp.bfloat16)
            far_copies[chunk][way].start()

    def project_near(chunk):
        rows = pl.ds(chunk * CHUNK, CHUNK)
        for way, to in ways:
            for at in range(2):
                place = 2 * (1 - way) + at
                near_sum[way, rows, tile(place)] = term(chunk, to, place).astype(jnp.bfloat16)
            near_copies[chunk][way][1 - way].start()

    def project_relay(chunk):
        rows = pl.ds(chunk * CHUNK, CHUNK)
        for way, to in ways:
            far_copies[chunk][way].wait_recv()
            for at in range(2):
                place = 2 * way + at
                near_sum[way, rows, tile(place)] = (
                    term(chunk, to, place) + far_landed[way, rows, tile(at)].astype(jnp.float32)
                ).astype(jnp.bfloat16)
            near_copies[chunk][way][way].start()

    def project_own(chunk):
        rows = pl.ds(chunk * CHUNK, CHUNK)
        for at in range(4):
            own[rows, tile(at)] = term(chunk, plane, at)

    order = (1, 0)
    for group in range(GROUPS):
        make_ready(group)
        if group < GROUPS - 1:
            for block in order:
                attend(block, group)
    loads[2 * GROUPS + 1].wait()
    for block in order:
        attend(block, GROUPS - 1)
        project_far(block)
        project_near(block)
    for chunk in order:
        project_relay(chunk)
    for chunk in order:
        project_own(chunk)
    for chunk in order:
        rows = pl.ds(chunk * CHUNK, CHUNK)
        for way in range(2):
            for at in range(2):
                near_copies[chunk][way][at].wait_recv()
        out_ref[rows, :] = (
            own[rows, :]
            + near_landed[0, rows, :].astype(jnp.float32)
            + near_landed[1, rows, :].astype(jnp.float32)
        ).astype(jnp.bfloat16)

    for chunk in order:
        for way in range(2):
            far_copies[chunk][way].wait_send()
            for at in range(2):
                near_copies[chunk][way][at].wait_send()
    for group in range(GROUPS):
        for name, condition in starts.items():
            if name == "two":
                condition = condition & first_core
            when(condition, copies[group][name].wait_send)


def per_device(query, key, value, out_weight):
    tokens = query.shape[0]
    dma = pltpu.SemaphoreType.DMA
    bf16 = jnp.bfloat16
    return pl.pallas_call(
        kernel,
        out_shape=pltpu.VMEM((tokens, WIDTH), bf16),
        in_specs=[pl.BlockSpec(memory_space=pl.ANY)] * 4,
        out_specs=pl.BlockSpec(memory_space=pltpu.VMEM),
        scratch_shapes=[
            pltpu.VMEM((GROUPS, 2, ROWS, SPAN), bf16),
            pltpu.VMEM((GROUPS, 2, 496, SPAN), bf16),
            pltpu.VMEM((GROUPS, 2, 64, SPAN), bf16),
            pltpu.VMEM((tokens, WIDTH), bf16),
            pltpu.VMEM((WIDTH, PLANES * WIDTH), bf16),
            pltpu.VMEM((tokens, WIDTH), bf16),
            pltpu.VMEM((2, tokens, WIDTH // 2), bf16),
            pltpu.VMEM((2, tokens, WIDTH), bf16),
            pltpu.VMEM((2, tokens, WIDTH // 2), bf16),
            pltpu.VMEM((2, tokens, WIDTH), bf16),
            pltpu.VMEM((tokens, WIDTH), jnp.float32),
            dma((2 * GROUPS + 2,)),
            dma((GROUPS, len(LINKS))),
            dma((GROUPS, len(LINKS))),
            dma((CHUNKS, 2, 1)),
            dma((CHUNKS, 2, 1)),
            dma((CHUNKS, 2, 2)),
            dma((CHUNKS, 2, 2)),
        ],
        compiler_params=pltpu.CompilerParams(
            collective_id=0, has_side_effects=True, vmem_limit_bytes=56 << 20
        ),
        cost_estimate=pl.CostEstimate(
            flops=8_000_000_000, bytes_accessed=13_000_000, transcendentals=7_400_000
        ),
        name="attend_and_project",
    )(query, key, value, out_weight)


def solution(mesh):
    in_specs = (P("seq", "head"), P("seq", "head"), P("seq", "head"), P("head", None))
    out_specs = P("seq", "head")
    return jax.shard_map(
        per_device, mesh=mesh, in_specs=in_specs, out_specs=out_specs, check_vma=False
    )
```

```python
import functools
import math

import jax
import jax.numpy as jnp
from jax import lax
from jax.experimental import pallas as pl
from jax.experimental.pallas import tpu as pltpu
from jax.sharding import PartitionSpec as P

DH = 128
B = 256
HALF = 128
WIDTH = 1024
GROUPS = 2
SPAN = WIDTH // GROUPS
HEADS = SPAN // DH
SIDE = 4
CHIPS = SIDE * SIDE
PLANES = 4
CHUNK = 256
CHUNKS = 2 * B // CHUNK
NEG = -1e30
SCALE = math.log2(math.e) / math.sqrt(DH)
MESH = pl.DeviceIdType.MESH


OWN = B
ROWS = 8 * B
LEVEL = {level: (2 + level) * B for level in range(1, 6)}
POOLED = {1: 0, 2: 256, 3: 384, 4: 448, 5: 480}
SHARED = ("two_s", "3a_s", "3b_s", "4a_s", "4b_s", "5a_s", "5b_s")
COLUMN = ("four_1", "four_2", "four_3", "five_1", "five_2", "five_3")
LINKS = ("tail", "first", "two", "three_1", "three_2", "four_x", "five_near", "five_far")
LINKS += COLUMN + SHARED


def aligned(at, unit):
    return pl.multiple_of(at, unit)


def kernel(
    q_hbm,
    k_hbm,
    v_hbm,
    w_hbm,
    out_ref,
    kv,
    pooled,
    gathered_five,
    q_ref,
    w_ref,
    attended,
    far_sum,
    near_sum,
    far_landed,
    near_landed,
    waiting,
    own,
    load_sem,
    link_send,
    link_recv,
    far_send,
    far_recv,
    near_send,
    near_recv,
):
    device = lax.axis_index("seq")
    plane = lax.axis_index("head")
    chip = device // 2
    core = device % 2
    x = chip // SIDE
    y = chip % SIDE

    def at_chip(chip_at):
        return jnp.clip(chip_at, 0, CHIPS - 1) * 2 + core

    def in_column(step):
        return (y + step) % SIDE

    odd = y % 2 == 1
    even = y % 2 == 0
    lower_half = y < 2
    upper_half = y >= 2
    sibling = 2 * chip + 1 - core
    above = (plane + 1) % PLANES
    below = (plane + 3) % PLANES
    across = (plane + 2) % PLANES
    first_core = core == 0
    second_core = core == 1
    three_first = (y == 0) | (y == 3) | (x >= 1)
    three_second = upper_half | (x >= 1)
    five_first = (x == SIDE - 1) | (x == 0)
    sees = {
        "3a": jnp.where(odd, three_first, three_second),
        "3b": jnp.where(odd, three_second, three_first),
        "4a": x >= 1,
        "4b": (x >= 1) & upper_half,
        "5a": x >= 2,
        "5b": (x == SIDE - 1) | (x == 0),
    }

    def column_needs(step):
        return (x >= 1) & (lower_half | (in_column(step) >= 2))

    def column_gives(step):
        return (x >= 1) & (upper_half | (in_column(-step) < 2))

    def when(condition, act):
        pl.when(condition)(act)

    loads = []
    for side, source in ((0, k_hbm), (1, v_hbm)):
        for group in range(GROUPS):
            loads.append(
                pltpu.make_async_copy(
                    source.at[:, pl.ds(group * SPAN, SPAN)],
                    kv.at[group, side, pl.ds(OWN, 2 * B)],
                    load_sem.at[len(loads)],
                )
            )
    loads.append(pltpu.make_async_copy(q_hbm, q_ref, load_sem.at[len(loads)]))
    loads.append(pltpu.make_async_copy(w_hbm, w_ref, load_sem.at[len(loads)]))
    for load in loads[: 2 * GROUPS]:
        load.start()

    barrier = pltpu.get_barrier_semaphore()

    def greet(seq_at, plane_at):
        pl.semaphore_signal(barrier, inc=1, device_id=(seq_at, plane_at), device_id_type=MESH)

    greet(device, above)
    greet(device, below)
    greet(sibling, plane)
    asked = 3

    def relation(from_there, source, to_there):
        when(from_there, lambda: greet(source, plane))
        return jnp.where(to_there, 1, 0)

    asked += relation(chip > 0, at_chip(chip - 1), chip < CHIPS - 1)
    asked += relation(
        first_core & (chip > 0),
        jnp.maximum(device - 1, 0),
        second_core & (chip < CHIPS - 1),
    )
    asked += relation(x > 0, at_chip(chip - SIDE), x < SIDE - 1)
    down = at_chip(x * SIDE + in_column(-1))
    three_to = at_chip(chip - 1 + jnp.where(upper_half, SIDE, jnp.where(y == 0, SIDE, 0)))
    three_from = at_chip(x * SIDE + in_column(1) - jnp.where((y == 1) | (y == 2), SIDE, 0))
    asked += relation(three_first, three_from, lower_half | (x < SIDE - 1))
    asked += relation(three_second, at_chip(x * SIDE + in_column(1)), three_first)
    for step in (1, 2, 3):
        asked += relation(
            (x < 2) | column_gives(step),
            at_chip(x * SIDE + in_column(-step)),
            (x < 2) | column_needs(step),
        )
    x_down = at_chip((x + 3) % SIDE * SIDE + y)
    asked += relation(x != 1, at_chip((x + 1) % SIDE * SIDE + y), x != 2)

    def pairs(rows):
        row = lax.broadcasted_iota(jnp.int32, (rows, 2 * rows), 0)
        col = lax.broadcasted_iota(jnp.int32, (rows, 2 * rows), 1)
        return jnp.where((col >> 1) == row, 0.5, 0.0).astype(jnp.bfloat16)

    def pool(half, rows):
        return jnp.dot(half, rows, preferred_element_type=jnp.float32).astype(jnp.bfloat16)

    for load in loads[: 2 * GROUPS]:
        load.wait()
    for load in loads[2 * GROUPS :]:
        load.start()

    tiles = [
        (group, side, pl.ds(at, 256))
        for group in range(GROUPS)
        for side in range(2)
        for at in range(0, SPAN, 256)
    ]
    half = pairs(HALF)
    for group, side, columns in tiles:
        for quarter in range(2):
            rows = kv[group, side, pl.ds(OWN + quarter * B, B), columns]
            pooled[group, side, pl.ds(quarter * HALF, HALF), columns] = pool(half, rows)
    for level in range(2, 6):
        count_out = 512 >> level
        half = pairs(count_out)
        for group, side, columns in tiles:
            rows = pooled[group, side, pl.ds(POOLED[level - 1], 2 * count_out), columns]
            rows = pool(half, rows)
            pooled[group, side, pl.ds(POOLED[level], count_out), columns] = rows
            if level == 5:
                gathered_five[group, side, pl.ds(aligned(y * 16, 16), 16), columns] = rows

    pl.semaphore_wait(barrier, asked)

    def link(name, group, source, target, to):
        return pltpu.make_async_remote_copy(
            src_ref=source,
            dst_ref=target,
            send_sem=link_send.at[group, LINKS.index(name)],
            recv_sem=link_recv.at[group, LINKS.index(name)],
            device_id=(to, plane),
            device_id_type=MESH,
        )

    def part(ref, group, start, rows):
        return ref.at[group, :, pl.ds(start, rows)]

    def same(name, group, ref, start, rows, to):
        piece = part(ref, group, start, rows)
        return link(name, group, piece, piece, to)

    def piece_at(level, half):
        return aligned(LEVEL[level] + half * HALF + core * 64, 64)

    def slot_four(at):
        return aligned(LEVEL[4] + at // 2 * HALF + core * 64 + at % 2 * 32, 32)

    def copies_of(group):
        c = {}
        to = jnp.where(first_core, sibling, jnp.minimum(device + 1, 2 * CHIPS - 1))
        tail = part(kv, group, OWN + B, B)
        c["tail"] = link("tail", group, tail, part(kv, group, 0, B), to)
        first = part(pooled, group, 0, HALF)
        c["first"] = link("first", group, first, part(kv, group, LEVEL[1], HALF), to)
        two = aligned(LEVEL[2] + core * HALF, HALF)
        source = part(pooled, group, POOLED[2], HALF)
        c["two"] = link("two", group, source, part(kv, group, two, HALF), at_chip(chip + 1))
        c["two_s"] = same("two_s", group, kv, two, HALF, sibling)
        three = part(pooled, group, POOLED[3], 64)
        target = part(kv, group, piece_at(3, y % 2), 64)
        c["three_1"] = link("three_1", group, three, target, three_to)
        c["three_2"] = same("three_2", group, kv, piece_at(3, 1 - y % 2), 64, down)
        four = part(pooled, group, POOLED[4], 32)
        target = part(kv, group, slot_four(y), 32)
        c["four_x"] = link("four_x", group, four, target, at_chip(chip + SIDE))
        slot = aligned(y * 16, 16)
        for step in (1, 2, 3):
            to = at_chip(x * SIDE + in_column(step))
            c[f"four_{step}"] = same(f"four_{step}", group, kv, slot_four(y), 32, to)
            c[f"five_{step}"] = same(f"five_{step}", group, gathered_five, slot, 16, to)
        target = part(kv, group, piece_at(5, jnp.where(x == 0, 0, 1)), 64)
        c["five_near"] = link("five_near", group, gathered_five.at[group], target, x_down)
        start = piece_at(5, jnp.where(x == 0, 1, 0))
        c["five_far"] = same("five_far", group, kv, start, 64, x_down)
        for name in sees:
            start = piece_at(int(name[0]), "ab".index(name[1]))
            c[name + "_s"] = same(name + "_s", group, kv, start, 64, sibling)
        return c

    copies = [copies_of(group) for group in range(GROUPS)]
    starts = [
        ("tail", device < 2 * CHIPS - 1),
        ("first", device < 2 * CHIPS - 1),
        ("two", chip < CHIPS - 1),
        ("three_1", lower_half | (x < SIDE - 1)),
        ("three_2", three_first),
        ("four_x", x < SIDE - 1),
        ("five_near", x < 2),
        ("five_far", five_first),
        ("two_s", chip > 0),
    ]
    for step in (1, 2, 3):
        starts.append((f"four_{step}", column_needs(step)))
        starts.append((f"five_{step}", x < 2))
    for name in sees:
        starts.append((name + "_s", sees[name]))
    starts = dict(starts)

    def begin(group, *names):
        for name in names:
            when(starts[name], copies[group][name].start)

    def arrived(group, name, condition):
        when(condition, copies[group][name].wait_recv)

    every = range(GROUPS)

    def send_first():
        for group in every:
            begin(group, "five_1", "five_3", "five_2", "four_x")
        for group in every:
            begin(group, "three_1")
        for group in every:
            begin(group, "two")

        @pl.when(first_core)
        def _():
            for group in every:
                copies[group]["tail"].start()
                copies[group]["first"].start()

    def send_second():
        for group in every:
            for step in (1, 2, 3):
                arrived(group, f"five_{step}", x < 2)
            begin(group, "five_near")
        for group in every:
            arrived(group, "four_x", x >= 1)
            begin(group, "four_1", "four_3", "four_2")
        for group in every:
            arrived(group, "three_1", three_first)
            begin(group, "three_2")
        for group in every:
            arrived(group, "five_near", five_first)
            begin(group, "five_far")

    def send_last(group):
        begin(group, "first", "tail")

    def pass_on(group):
        arrived(group, "three_2", three_second)
        begin(group, "3a_s", "3b_s")
        for step in (1, 2, 3):
            arrived(group, f"four_{step}", column_gives(step))
        begin(group, "4a_s", "4b_s")
        arrived(group, "two", chip > 0)
        begin(group, "two_s")
        arrived(group, "five_far", x >= 2)
        begin(group, "5a_s", "5b_s")

    def ready(group):
        for name in sees:
            arrived(group, name + "_s", sees[name])
        arrived(group, "two_s", chip > 0)
        arrived(group, "first", (device > 0))
        arrived(group, "tail", (device > 0))
        half = pairs(HALF)
        for at, side, columns in tiles:
            if at == group:
                kv[group, side, pl.ds(LEVEL[1] + HALF, HALF), columns] = pool(
                    half, kv[group, side, pl.ds(0, B), columns]
                )

    send_first()

    def clear(start, rows):
        kv[:, :, pl.ds(start, rows), :] = jnp.zeros((GROUPS, 2, rows, SPAN), jnp.bfloat16)

    @pl.when(device == 0)
    def _():
        clear(0, B)
        clear(LEVEL[1], HALF)

    @pl.when(chip == 0)
    def _():
        clear(LEVEL[2], B)

    for name in sees:
        when(
            jnp.logical_not(sees[name]),
            functools.partial(clear, LEVEL[int(name[0])] + "ab".index(name[1]) * HALF, HALF),
        )

    send_second()

    @pl.when(second_core)
    def _():
        for group in range(GROUPS):
            when(starts["two"], copies[group]["two"].wait_send)
        for group in range(GROUPS):
            send_last(group)

    @pl.when(first_core)
    def _():
        for group in range(GROUPS):
            pass_on(group)

    def make_ready(group):
        when(second_core, functools.partial(pass_on, group))
        ready(group)

    loads[2 * GROUPS].wait()

    def nt(left, right):
        return lax.dot_general(
            left, right, (((1,), (1,)), ((), ())), preferred_element_type=jnp.float32
        )

    past = lax.broadcasted_iota(jnp.int32, (HALF, HALF), 0) <= lax.broadcasted_iota(
        jnp.int32, (HALF, HALF), 1
    )

    def block_parts(block):
        beta = 2 * device + block
        prior = jnp.where(beta >= 1, 0.0, NEG) if block == 0 else None
        biases = [prior, prior, None, None]
        for level in range(1, 6):
            there = beta // 2**level >= 1
            whole = there & (beta // 2 ** (level - 1) % 2 == 1)
            biases.append(jnp.where(there, float(level), NEG))
            biases.append(jnp.where(whole, float(level), NEG))
        return [block * B, block * B + B] + [LEVEL[level] for level in range(1, 6)], biases

    def scores(block, group, head):
        starts, biases = block_parts(block)
        columns = pl.ds(head * DH, DH)
        queries = q_ref[pl.ds(block * B, B), pl.ds(group * SPAN + head * DH, DH)]
        halves = []
        peak = None
        for at, start in enumerate(starts):
            dots = nt(kv[group, 0, pl.ds(start, B), columns], queries)
            top, low = dots[:HALF], dots[HALF:]
            if at == 1:
                top = jnp.concatenate(
                    [jnp.where(past, top[:, :HALF], NEG), top[:, HALF:]], 1
                )
                low = jnp.concatenate(
                    [jnp.full((HALF, HALF), NEG), jnp.where(past, low[:, HALF:], NEG)], 1
                )
            for dots, bias in zip((top, low), biases[2 * at : 2 * at + 2]):
                high = jnp.max(dots, axis=0, keepdims=True) * SCALE
                if bias is not None:
                    high = high + bias
                peak = high if peak is None else jnp.maximum(peak, high)
                halves.append(dots)
        return halves, peak

    def average(block, group, head, halves, peak):
        starts, biases = block_parts(block)
        columns = pl.ds(head * DH, DH)
        total = jnp.zeros((1, B), jnp.float32)
        summed = jnp.zeros((DH, B), jnp.float32)
        probs = []
        for at in range(len(starts)):
            weights = []
            for dots, bias in zip(halves[2 * at : 2 * at + 2], biases[2 * at : 2 * at + 2]):
                shift = peak if bias is None else peak - bias
                weights.append(jnp.exp2(dots * SCALE - shift))
            weights = jnp.concatenate(weights, 0)
            total = total + jnp.sum(weights, axis=0, keepdims=True)
            probs.append(weights.astype(jnp.bfloat16))
            if at == 1 or at == len(starts) - 1:
                start = starts[at + 1 - len(probs)]
                values = jnp.transpose(kv[group, 1, pl.ds(start, B * len(probs)), columns])
                summed = summed + jnp.dot(
                    values, jnp.concatenate(probs, 0), preferred_element_type=jnp.float32
                )
                probs = []
        attended[pl.ds(block * B, B), pl.ds(group * SPAN + head * DH, DH)] = jnp.transpose(
            summed / total
        ).astype(jnp.bfloat16)

    def attend(*block_groups):
        before = None
        for block, group in block_groups:
            for head in range(HEADS):
                ahead = (block, group, head, *scores(block, group, head))
                if before is not None:
                    average(*before)
                before = ahead
        average(*before)

    def term(chunk, target, at):
        columns = pl.ds(aligned(target * WIDTH + at * 256, 256), 256)
        return jnp.dot(
            attended[pl.ds(chunk * CHUNK, CHUNK), :],
            w_ref[:, columns],
            preferred_element_type=jnp.float32,
        )

    def sends(send, recv, source, landed, chunk, way, to, at):
        rows = pl.ds(chunk * CHUNK, CHUNK)
        columns = pl.ds(at * 512, 512)
        return pltpu.make_async_remote_copy(
            src_ref=source.at[way, rows, columns],
            dst_ref=landed.at[way, rows, columns],
            send_sem=send.at[chunk, way, at],
            recv_sem=recv.at[chunk, way, at],
            device_id=(device, to),
            device_id_type=MESH,
        )

    ways = ((0, above), (1, below))
    far_copies = [
        [sends(far_send, far_recv, far_sum, far_landed, chunk, way, to, 0) for way, to in ways]
        for chunk in range(CHUNKS)
    ]
    near_copies = [
        [
            [sends(near_send, near_recv, near_sum, near_landed, chunk, way, to, at) for at in range(2)]
            for way, to in ways
        ]
        for chunk in range(CHUNKS)
    ]

    def tile(at):
        return pl.ds(at * 256, 256)

    def project_far(chunk):
        rows = pl.ds(chunk * CHUNK, CHUNK)
        for way in range(2):
            for at in range(2):
                far_sum[way, rows, tile(at)] = term(chunk, across, 2 * way + at).astype(jnp.bfloat16)
            far_copies[chunk][way].start()

    def project_near(chunk):
        rows = pl.ds(chunk * CHUNK, CHUNK)
        for way, to in ways:
            for at in range(2):
                place = 2 * (1 - way) + at
                near_sum[way, rows, tile(place)] = term(chunk, to, place).astype(jnp.bfloat16)
            near_copies[chunk][way][1 - way].start()

    def prepare_relay(chunk):
        rows = pl.ds(chunk * CHUNK, CHUNK)
        for way, to in ways:
            for at in range(2):
                waiting[way, rows, tile(at)] = term(chunk, to, 2 * way + at)

    def send_relay(chunk):
        rows = pl.ds(chunk * CHUNK, CHUNK)
        for way, to in ways:
            far_copies[chunk][way].wait_recv()
            columns = pl.ds(way * 512, 512)
            near_sum[way, rows, columns] = (
                waiting[way, rows, :] + far_landed[way, rows, :].astype(jnp.float32)
            ).astype(jnp.bfloat16)
            near_copies[chunk][way][way].start()

    def project_own(chunk):
        rows = pl.ds(chunk * CHUNK, CHUNK)
        for at in range(4):
            own[rows, tile(at)] = term(chunk, plane, at)

    order = (1, 0)
    make_ready(0)

    attend((1, 0), (0, 0))
    make_ready(1)
    loads[2 * GROUPS + 1].wait()
    attend((1, 1))
    project_far(1)
    project_near(1)

    attend((0, 1))
    project_far(0)

    prepare_relay(1)
    send_relay(1)
    project_near(0)
    prepare_relay(0)
    project_own(1)
    project_own(0)
    send_relay(0)
    for chunk in order:
        rows = pl.ds(chunk * CHUNK, CHUNK)
        for way in range(2):
            for at in range(2):
                near_copies[chunk][way][at].wait_recv()
        out_ref[rows, :] = (
            own[rows, :]
            + near_landed[0, rows, :].astype(jnp.float32)
            + near_landed[1, rows, :].astype(jnp.float32)
        ).astype(jnp.bfloat16)

    for chunk in order:
        for way in range(2):
            far_copies[chunk][way].wait_send()
            for at in range(2):
                near_copies[chunk][way][at].wait_send()
    for group in range(GROUPS):
        for name, condition in starts.items():
            if name == "two":
                condition = condition & first_core
            when(condition, copies[group][name].wait_send)


def per_device(query, key, value, out_weight):
    tokens = query.shape[0]
    dma = pltpu.SemaphoreType.DMA
    bf16 = jnp.bfloat16
    return pl.pallas_call(
        kernel,
        out_shape=pltpu.VMEM((tokens, WIDTH), bf16),
        in_specs=[pl.BlockSpec(memory_space=pl.ANY)] * 4,
        out_specs=pl.BlockSpec(memory_space=pltpu.VMEM),
        scratch_shapes=[
            pltpu.VMEM((GROUPS, 2, ROWS, SPAN), bf16),
            pltpu.VMEM((GROUPS, 2, 496, SPAN), bf16),
            pltpu.VMEM((GROUPS, 2, 64, SPAN), bf16),
            pltpu.VMEM((tokens, WIDTH), bf16),
            pltpu.VMEM((WIDTH, PLANES * WIDTH), bf16),
            pltpu.VMEM((tokens, WIDTH), bf16),
            pltpu.VMEM((2, tokens, WIDTH // 2), bf16),
            pltpu.VMEM((2, tokens, WIDTH), bf16),
            pltpu.VMEM((2, tokens, WIDTH // 2), bf16),
            pltpu.VMEM((2, tokens, WIDTH), bf16),
            pltpu.VMEM((2, tokens, WIDTH // 2), jnp.float32),
            pltpu.VMEM((tokens, WIDTH), jnp.float32),
            dma((2 * GROUPS + 2,)),
            dma((GROUPS, len(LINKS))),
            dma((GROUPS, len(LINKS))),
            dma((CHUNKS, 2, 1)),
            dma((CHUNKS, 2, 1)),
            dma((CHUNKS, 2, 2)),
            dma((CHUNKS, 2, 2)),
        ],
        compiler_params=pltpu.CompilerParams(
            collective_id=0, has_side_effects=True, vmem_limit_bytes=56 << 20
        ),
        cost_estimate=pl.CostEstimate(
            flops=8_000_000_000, bytes_accessed=13_000_000, transcendentals=7_400_000
        ),
        name="attend_and_project",
    )(query, key, value, out_weight)


def solution(mesh):
    in_specs = (P("seq", "head"), P("seq", "head"), P("seq", "head"), P("head", None))
    out_specs = P("seq", "head")
    return jax.shard_map(
        per_device, mesh=mesh, in_specs=in_specs, out_specs=out_specs, check_vma=False
    )
```

```python
import functools
import math

import jax
import jax.numpy as jnp
from jax import lax
from jax.experimental import pallas as pl
from jax.experimental.pallas import tpu as pltpu
from jax.sharding import PartitionSpec as P

DH = 128
B = 256
HALF = 128
WIDTH = 1024
GROUPS = 2
SPAN = WIDTH // GROUPS
HEADS = SPAN // DH
SIDE = 4
CHIPS = SIDE * SIDE
PLANES = 4
CHUNK = 256
CHUNKS = 2 * B // CHUNK
NEG = -1e30
SCALE = math.log2(math.e) / math.sqrt(DH)
MESH = pl.DeviceIdType.MESH


OWN = B
ROWS = 8 * B
LEVEL = {level: (2 + level) * B for level in range(1, 6)}
POOLED = {1: 0, 2: 256, 3: 384, 4: 448, 5: 480}
SHARED = ("two_s", "3a_s", "3b_s", "4a_s", "4b_s", "5a_s", "5b_s")
COLUMN = ("four_1", "four_2", "four_3", "five_1", "five_2", "five_3")
LINKS = ("tail", "first", "two", "three_1", "three_2", "four_x", "five_near", "five_far")
LINKS += COLUMN + SHARED


def aligned(at, unit):
    return pl.multiple_of(at, unit)


def kernel(
    q_hbm,
    k_hbm,
    v_hbm,
    w_hbm,
    out_ref,
    kv,
    pooled,
    gathered_five,
    q_ref,
    w_ref,
    attended,
    far_sum,
    near_sum,
    far_landed,
    near_landed,
    waiting,
    own,
    load_sem,
    link_send,
    link_recv,
    far_send,
    far_recv,
    near_send,
    near_recv,
):
    device = lax.axis_index("seq")
    plane = lax.axis_index("head")
    chip = device // 2
    core = device % 2
    x = chip // SIDE
    y = chip % SIDE

    def at_chip(chip_at):
        return jnp.clip(chip_at, 0, CHIPS - 1) * 2 + core

    def in_column(step):
        return (y + step) % SIDE

    odd = y % 2 == 1
    even = y % 2 == 0
    lower_half = y < 2
    upper_half = y >= 2
    sibling = 2 * chip + 1 - core
    above = (plane + 1) % PLANES
    below = (plane + 3) % PLANES
    across = (plane + 2) % PLANES
    first_core = core == 0
    second_core = core == 1
    three_first = (y == 0) | (y == 3) | (x >= 1)
    three_second = upper_half | (x >= 1)
    five_first = (x == SIDE - 1) | (x == 0)
    sees = {
        "3a": jnp.where(odd, three_first, three_second),
        "3b": jnp.where(odd, three_second, three_first),
        "4a": x >= 1,
        "4b": (x >= 1) & upper_half,
        "5a": x >= 2,
        "5b": (x == SIDE - 1) | (x == 0),
    }

    def column_needs(step):
        return (x >= 1) & (lower_half | (in_column(step) >= 2))

    def column_gives(step):
        return (x >= 1) & (upper_half | (in_column(-step) < 2))

    def when(condition, act):
        pl.when(condition)(act)

    loads = []
    for side, source in ((0, k_hbm), (1, v_hbm)):
        for group in range(GROUPS):
            loads.append(
                pltpu.make_async_copy(
                    source.at[:, pl.ds(group * SPAN, SPAN)],
                    kv.at[group, side, pl.ds(OWN, 2 * B)],
                    load_sem.at[len(loads)],
                )
            )
    loads.append(pltpu.make_async_copy(q_hbm, q_ref, load_sem.at[len(loads)]))
    loads.append(pltpu.make_async_copy(w_hbm, w_ref, load_sem.at[len(loads)]))
    for load in loads[: 2 * GROUPS]:
        load.start()

    barrier = pltpu.get_barrier_semaphore()

    def greet(seq_at, plane_at):
        pl.semaphore_signal(barrier, inc=1, device_id=(seq_at, plane_at), device_id_type=MESH)

    greet(device, above)
    greet(device, below)
    greet(sibling, plane)
    asked = 3

    def relation(from_there, source, to_there):
        when(from_there, lambda: greet(source, plane))
        return jnp.where(to_there, 1, 0)

    asked += relation(chip > 0, at_chip(chip - 1), chip < CHIPS - 1)
    asked += relation(
        first_core & (chip > 0),
        jnp.maximum(device - 1, 0),
        second_core & (chip < CHIPS - 1),
    )
    asked += relation(x > 0, at_chip(chip - SIDE), x < SIDE - 1)
    down = at_chip(x * SIDE + in_column(-1))
    three_to = at_chip(chip - 1 + jnp.where(upper_half, SIDE, jnp.where(y == 0, SIDE, 0)))
    three_from = at_chip(x * SIDE + in_column(1) - jnp.where((y == 1) | (y == 2), SIDE, 0))
    asked += relation(three_first, three_from, lower_half | (x < SIDE - 1))
    asked += relation(three_second, at_chip(x * SIDE + in_column(1)), three_first)
    for step in (1, 2, 3):
        asked += relation(
            (x < 2) | column_gives(step),
            at_chip(x * SIDE + in_column(-step)),
            (x < 2) | column_needs(step),
        )
    x_down = at_chip((x + 3) % SIDE * SIDE + y)
    asked += relation(x != 1, at_chip((x + 1) % SIDE * SIDE + y), x != 2)

    def pairs(rows):
        row = lax.broadcasted_iota(jnp.int32, (rows, 2 * rows), 0)
        col = lax.broadcasted_iota(jnp.int32, (rows, 2 * rows), 1)
        return jnp.where((col >> 1) == row, 0.5, 0.0).astype(jnp.bfloat16)

    def pool(half, rows):
        return jnp.dot(half, rows, preferred_element_type=jnp.float32).astype(jnp.bfloat16)

    for load in loads[: 2 * GROUPS]:
        load.wait()
    for load in loads[2 * GROUPS :]:
        load.start()

    tiles = [
        (group, side, pl.ds(at, 256))
        for group in range(GROUPS)
        for side in range(2)
        for at in range(0, SPAN, 256)
    ]
    half = pairs(HALF)
    for group, side, columns in tiles:
        for quarter in range(2):
            rows = kv[group, side, pl.ds(OWN + quarter * B, B), columns]
            pooled[group, side, pl.ds(quarter * HALF, HALF), columns] = pool(half, rows)
    for level in range(2, 6):
        count_out = 512 >> level
        half = pairs(count_out)
        for group, side, columns in tiles:
            rows = pooled[group, side, pl.ds(POOLED[level - 1], 2 * count_out), columns]
            rows = pool(half, rows)
            pooled[group, side, pl.ds(POOLED[level], count_out), columns] = rows
            if level == 5:
                gathered_five[group, side, pl.ds(aligned(y * 16, 16), 16), columns] = rows

    pl.semaphore_wait(barrier, asked)

    def link(name, group, source, target, to):
        return pltpu.make_async_remote_copy(
            src_ref=source,
            dst_ref=target,
            send_sem=link_send.at[group, LINKS.index(name)],
            recv_sem=link_recv.at[group, LINKS.index(name)],
            device_id=(to, plane),
            device_id_type=MESH,
        )

    def part(ref, group, start, rows):
        return ref.at[group, :, pl.ds(start, rows)]

    def same(name, group, ref, start, rows, to):
        piece = part(ref, group, start, rows)
        return link(name, group, piece, piece, to)

    def piece_at(level, half):
        return aligned(LEVEL[level] + half * HALF + core * 64, 64)

    def slot_four(at):
        return aligned(LEVEL[4] + at // 2 * HALF + core * 64 + at % 2 * 32, 32)

    def copies_of(group):
        c = {}
        to = jnp.where(first_core, sibling, jnp.minimum(device + 1, 2 * CHIPS - 1))
        tail = part(kv, group, OWN + B, B)
        c["tail"] = link("tail", group, tail, part(kv, group, 0, B), to)
        first = part(pooled, group, 0, HALF)
        c["first"] = link("first", group, first, part(kv, group, LEVEL[1], HALF), to)
        two = aligned(LEVEL[2] + core * HALF, HALF)
        source = part(pooled, group, POOLED[2], HALF)
        c["two"] = link("two", group, source, part(kv, group, two, HALF), at_chip(chip + 1))
        c["two_s"] = same("two_s", group, kv, two, HALF, sibling)
        three = part(pooled, group, POOLED[3], 64)
        target = part(kv, group, piece_at(3, y % 2), 64)
        c["three_1"] = link("three_1", group, three, target, three_to)
        c["three_2"] = same("three_2", group, kv, piece_at(3, 1 - y % 2), 64, down)
        four = part(pooled, group, POOLED[4], 32)
        target = part(kv, group, slot_four(y), 32)
        c["four_x"] = link("four_x", group, four, target, at_chip(chip + SIDE))
        slot = aligned(y * 16, 16)
        for step in (1, 2, 3):
            to = at_chip(x * SIDE + in_column(step))
            c[f"four_{step}"] = same(f"four_{step}", group, kv, slot_four(y), 32, to)
            c[f"five_{step}"] = same(f"five_{step}", group, gathered_five, slot, 16, to)
        target = part(kv, group, piece_at(5, jnp.where(x == 0, 0, 1)), 64)
        c["five_near"] = link("five_near", group, gathered_five.at[group], target, x_down)
        start = piece_at(5, jnp.where(x == 0, 1, 0))
        c["five_far"] = same("five_far", group, kv, start, 64, x_down)
        for name in sees:
            start = piece_at(int(name[0]), "ab".index(name[1]))
            c[name + "_s"] = same(name + "_s", group, kv, start, 64, sibling)
        return c

    copies = [copies_of(group) for group in range(GROUPS)]
    starts = [
        ("tail", device < 2 * CHIPS - 1),
        ("first", device < 2 * CHIPS - 1),
        ("two", chip < CHIPS - 1),
        ("three_1", lower_half | (x < SIDE - 1)),
        ("three_2", three_first),
        ("four_x", x < SIDE - 1),
        ("five_near", x < 2),
        ("five_far", five_first),
        ("two_s", chip > 0),
    ]
    for step in (1, 2, 3):
        starts.append((f"four_{step}", column_needs(step)))
        starts.append((f"five_{step}", x < 2))
    for name in sees:
        starts.append((name + "_s", sees[name]))
    starts = dict(starts)

    def begin(group, *names):
        for name in names:
            when(starts[name], copies[group][name].start)

    def arrived(group, name, condition):
        when(condition, copies[group][name].wait_recv)

    every = range(GROUPS)

    def send_first():
        for group in every:
            begin(group, "five_1", "five_3", "five_2", "four_x")
        for group in every:
            begin(group, "three_1")
        for group in every:
            begin(group, "two")

        @pl.when(first_core)
        def _():
            for group in every:
                copies[group]["tail"].start()
                copies[group]["first"].start()

    def send_second():
        for group in every:
            for step in (1, 2, 3):
                arrived(group, f"five_{step}", x < 2)
            begin(group, "five_near")
        for group in every:
            arrived(group, "four_x", x >= 1)
            begin(group, "four_1", "four_3", "four_2")
        for group in every:
            arrived(group, "three_1", three_first)
            begin(group, "three_2")
        for group in every:
            arrived(group, "five_near", five_first)
            begin(group, "five_far")

    def send_last(group):
        begin(group, "first", "tail")

    def pass_on(group):
        arrived(group, "three_2", three_second)
        begin(group, "3a_s", "3b_s")
        for step in (1, 2, 3):
            arrived(group, f"four_{step}", column_gives(step))
        begin(group, "4a_s", "4b_s")
        arrived(group, "two", chip > 0)
        begin(group, "two_s")
        arrived(group, "five_far", x >= 2)
        begin(group, "5a_s", "5b_s")

    def ready(group):
        for name in sees:
            arrived(group, name + "_s", sees[name])
        arrived(group, "two_s", chip > 0)
        arrived(group, "first", (device > 0))
        arrived(group, "tail", (device > 0))
        half = pairs(HALF)
        for at, side, columns in tiles:
            if at == group:
                kv[group, side, pl.ds(LEVEL[1] + HALF, HALF), columns] = pool(
                    half, kv[group, side, pl.ds(0, B), columns]
                )

    send_first()

    def clear(start, rows):
        kv[:, :, pl.ds(start, rows), :] = jnp.zeros((GROUPS, 2, rows, SPAN), jnp.bfloat16)

    @pl.when(device == 0)
    def _():
        clear(0, B)
        clear(LEVEL[1], HALF)

    @pl.when(chip == 0)
    def _():
        clear(LEVEL[2], B)

    for name in sees:
        when(
            jnp.logical_not(sees[name]),
            functools.partial(clear, LEVEL[int(name[0])] + "ab".index(name[1]) * HALF, HALF),
        )

    send_second()

    @pl.when(second_core)
    def _():
        for group in range(GROUPS):
            when(starts["two"], copies[group]["two"].wait_send)
        for group in range(GROUPS):
            send_last(group)

    @pl.when(first_core)
    def _():
        for group in range(GROUPS):
            pass_on(group)

    def make_ready(group):
        when(second_core, functools.partial(pass_on, group))
        ready(group)

    loads[2 * GROUPS].wait()

    def nt(left, right):
        return lax.dot_general(
            left, right, (((1,), (1,)), ((), ())), preferred_element_type=jnp.float32
        )

    past = lax.broadcasted_iota(jnp.int32, (HALF, HALF), 0) <= lax.broadcasted_iota(
        jnp.int32, (HALF, HALF), 1
    )

    def block_parts(block):
        beta = 2 * device + block
        prior = jnp.where(beta >= 1, 0.0, NEG) if block == 0 else None
        biases = [prior, prior, None, None]
        for level in range(1, 6):
            there = beta // 2**level >= 1
            whole = there & (beta // 2 ** (level - 1) % 2 == 1)
            biases.append(jnp.where(there, float(level), NEG))
            biases.append(jnp.where(whole, float(level), NEG))
        return [block * B, block * B + B] + [LEVEL[level] for level in range(1, 6)], biases

    def scores(block, group, head):
        starts, biases = block_parts(block)
        columns = pl.ds(head * DH, DH)
        queries = q_ref[pl.ds(block * B, B), pl.ds(group * SPAN + head * DH, DH)]
        halves = []
        peak = None
        for at, start in enumerate(starts):
            unseen = block == 0 and at == 2
            dots = nt(kv[group, 0, pl.ds(start, HALF if unseen else B), columns], queries)
            top, low = dots[:HALF], None if unseen else dots[HALF:]
            if at == 1:
                top = jnp.concatenate(
                    [jnp.where(past, top[:, :HALF], NEG), top[:, HALF:]], 1
                )
                low = jnp.concatenate(
                    [jnp.full((HALF, HALF), NEG), jnp.where(past, low[:, HALF:], NEG)], 1
                )
            for dots, bias in zip((top, low), biases[2 * at : 2 * at + 2]):
                if dots is None:
                    halves.append(None)
                    continue
                high = jnp.max(dots, axis=0, keepdims=True) * SCALE
                if bias is not None:
                    high = high + bias
                peak = high if peak is None else jnp.maximum(peak, high)
                halves.append(dots)
        return halves, peak

    def average(block, group, head, halves, peak):
        starts, biases = block_parts(block)
        columns = pl.ds(head * DH, DH)
        total = jnp.zeros((1, B), jnp.float32)
        summed = jnp.zeros((DH, B), jnp.float32)
        probs = []
        for at in range(len(starts)):
            weights = []
            for dots, bias in zip(halves[2 * at : 2 * at + 2], biases[2 * at : 2 * at + 2]):
                if dots is None:
                    weights.append(jnp.zeros((HALF, B), jnp.float32))
                    continue
                shift = peak if bias is None else peak - bias
                if at == 1 and len(weights) == 1:
                    late = jnp.exp2(dots[:, HALF:] * SCALE - shift[:, HALF:])
                    weights.append(jnp.concatenate([jnp.zeros((HALF, HALF), jnp.float32), late], 1))
                    continue
                weights.append(jnp.exp2(dots * SCALE - shift))
            weights = jnp.concatenate(weights, 0)
            total = total + jnp.sum(weights, axis=0, keepdims=True)
            probs.append(weights.astype(jnp.bfloat16))
            if at == 1 or at == len(starts) - 1:
                start = starts[at + 1 - len(probs)]
                values = jnp.transpose(kv[group, 1, pl.ds(start, B * len(probs)), columns])
                summed = summed + jnp.dot(
                    values, jnp.concatenate(probs, 0), preferred_element_type=jnp.float32
                )
                probs = []
        attended[pl.ds(block * B, B), pl.ds(group * SPAN + head * DH, DH)] = jnp.transpose(
            summed / total
        ).astype(jnp.bfloat16)

    def attend(*block_groups):
        before = None
        for block, group in block_groups:
            for head in range(HEADS):
                ahead = (block, group, head, *scores(block, group, head))
                if before is not None:
                    average(*before)
                before = ahead
        average(*before)

    def term(chunk, target, at):
        columns = pl.ds(aligned(target * WIDTH + at * 256, 256), 256)
        return jnp.dot(
            attended[pl.ds(chunk * CHUNK, CHUNK), :],
            w_ref[:, columns],
            preferred_element_type=jnp.float32,
        )

    def sends(send, recv, source, landed, chunk, way, to, at):
        rows = pl.ds(chunk * CHUNK, CHUNK)
        columns = pl.ds(at * 512, 512)
        return pltpu.make_async_remote_copy(
            src_ref=source.at[way, rows, columns],
            dst_ref=landed.at[way, rows, columns],
            send_sem=send.at[chunk, way, at],
            recv_sem=recv.at[chunk, way, at],
            device_id=(device, to),
            device_id_type=MESH,
        )

    ways = ((0, above), (1, below))
    far_copies = [
        [sends(far_send, far_recv, far_sum, far_landed, chunk, way, to, 0) for way, to in ways]
        for chunk in range(CHUNKS)
    ]
    near_copies = [
        [
            [sends(near_send, near_recv, near_sum, near_landed, chunk, way, to, at) for at in range(2)]
            for way, to in ways
        ]
        for chunk in range(CHUNKS)
    ]

    def tile(at):
        return pl.ds(at * 256, 256)

    def project_far(chunk):
        rows = pl.ds(chunk * CHUNK, CHUNK)
        for way in range(2):
            for at in range(2):
                far_sum[way, rows, tile(at)] = term(chunk, across, 2 * way + at).astype(jnp.bfloat16)
            far_copies[chunk][way].start()

    def project_near(chunk):
        rows = pl.ds(chunk * CHUNK, CHUNK)
        for way, to in ways:
            for at in range(2):
                place = 2 * (1 - way) + at
                near_sum[way, rows, tile(place)] = term(chunk, to, place).astype(jnp.bfloat16)
            near_copies[chunk][way][1 - way].start()

    def prepare_relay(chunk):
        rows = pl.ds(chunk * CHUNK, CHUNK)
        for way, to in ways:
            for at in range(2):
                waiting[way, rows, tile(at)] = term(chunk, to, 2 * way + at)

    def send_relay(chunk):
        rows = pl.ds(chunk * CHUNK, CHUNK)
        for way, to in ways:
            far_copies[chunk][way].wait_recv()
            columns = pl.ds(way * 512, 512)
            near_sum[way, rows, columns] = (
                waiting[way, rows, :] + far_landed[way, rows, :].astype(jnp.float32)
            ).astype(jnp.bfloat16)
            near_copies[chunk][way][way].start()

    def project_own(chunk):
        rows = pl.ds(chunk * CHUNK, CHUNK)
        for at in range(4):
            own[rows, tile(at)] = term(chunk, plane, at)

    order = (1, 0)
    make_ready(0)

    attend((1, 0), (0, 0))
    make_ready(1)
    loads[2 * GROUPS + 1].wait()
    attend((1, 1))
    project_far(1)
    project_near(1)

    attend((0, 1))
    project_far(0)

    prepare_relay(1)
    send_relay(1)
    project_near(0)
    prepare_relay(0)
    project_own(1)
    project_own(0)
    send_relay(0)
    for chunk in order:
        rows = pl.ds(chunk * CHUNK, CHUNK)
        for way in range(2):
            for at in range(2):
                near_copies[chunk][way][at].wait_recv()
        out_ref[rows, :] = (
            own[rows, :]
            + near_landed[0, rows, :].astype(jnp.float32)
            + near_landed[1, rows, :].astype(jnp.float32)
        ).astype(jnp.bfloat16)

    for chunk in order:
        for way in range(2):
            far_copies[chunk][way].wait_send()
            for at in range(2):
                near_copies[chunk][way][at].wait_send()
    for group in range(GROUPS):
        for name, condition in starts.items():
            if name == "two":
                condition = condition & first_core
            when(condition, copies[group][name].wait_send)


def per_device(query, key, value, out_weight):
    tokens = query.shape[0]
    dma = pltpu.SemaphoreType.DMA
    bf16 = jnp.bfloat16
    return pl.pallas_call(
        kernel,
        out_shape=pltpu.VMEM((tokens, WIDTH), bf16),
        in_specs=[pl.BlockSpec(memory_space=pl.ANY)] * 4,
        out_specs=pl.BlockSpec(memory_space=pltpu.VMEM),
        scratch_shapes=[
            pltpu.VMEM((GROUPS, 2, ROWS, SPAN), bf16),
            pltpu.VMEM((GROUPS, 2, 496, SPAN), bf16),
            pltpu.VMEM((GROUPS, 2, 64, SPAN), bf16),
            pltpu.VMEM((tokens, WIDTH), bf16),
            pltpu.VMEM((WIDTH, PLANES * WIDTH), bf16),
            pltpu.VMEM((tokens, WIDTH), bf16),
            pltpu.VMEM((2, tokens, WIDTH // 2), bf16),
            pltpu.VMEM((2, tokens, WIDTH), bf16),
            pltpu.VMEM((2, tokens, WIDTH // 2), bf16),
            pltpu.VMEM((2, tokens, WIDTH), bf16),
            pltpu.VMEM((2, tokens, WIDTH // 2), jnp.float32),
            pltpu.VMEM((tokens, WIDTH), jnp.float32),
            dma((2 * GROUPS + 2,)),
            dma((GROUPS, len(LINKS))),
            dma((GROUPS, len(LINKS))),
            dma((CHUNKS, 2, 1)),
            dma((CHUNKS, 2, 1)),
            dma((CHUNKS, 2, 2)),
            dma((CHUNKS, 2, 2)),
        ],
        compiler_params=pltpu.CompilerParams(
            collective_id=0, has_side_effects=True, vmem_limit_bytes=56 << 20
        ),
        cost_estimate=pl.CostEstimate(
            flops=8_000_000_000, bytes_accessed=13_000_000, transcendentals=7_400_000
        ),
        name="attend_and_project",
    )(query, key, value, out_weight)


def solution(mesh):
    in_specs = (P("seq", "head"), P("seq", "head"), P("seq", "head"), P("head", None))
    out_specs = P("seq", "head")
    return jax.shard_map(
        per_device, mesh=mesh, in_specs=in_specs, out_specs=out_specs, check_vma=False
    )
```
